32 devices in a mesh: grp: 2 (over y), node: 16 (over z, x, core).
Axes of the slice: x: 2, y: 2, z: 4, core: 2. Of those that a mesh axis runs over, the one named last changes fastest.
Arguments:
- tokens: bfloat16 [128, 7168], P(('grp', 'node')), parts along dimension 0, may hold values from -6 to 6
- routes: int32 [128, 2], P(('grp', 'node')), parts along dimension 0, may hold values from 0 to 3, all different within a row; in each aligned block of 4 rows (0 to 3, 4 to 7, ...) at most 4 rows name the same one
- gates: float32 [128, 2], P(('grp', 'node')), parts along dimension 0, may hold values from 0.05 to 1
- norm_gain: bfloat16 [7168], replicated, may hold values from 0.5 to 1.5
- w_gate: bfloat16 [16, 7168, 256], P('node'), may hold values from -0.0625 to 0.0625
- w_up: bfloat16 [16, 7168, 256], P('node'), may hold values from -0.0625 to 0.0625
- w_down: bfloat16 [16, 256, 7168], P('node'), may hold values from -0.1875 to 0.1875
- queries: bfloat16 [32, 128, 576], P(('grp', 'node')), parts along dimension 0, may hold values from -60 to 60
- cache: bfloat16 [32, 1280, 576], P(('grp', 'node')), parts along dimension 0, may hold values from -6 to 6
- lengths: int32 [32], P(('grp', 'node')), parts along dimension 0, may hold values from 1 to 1280, as said below
Outputs:
- moe_out: bfloat16 [128, 7168], P(('grp', 'node')), parts along dimension 0
- attention_out: bfloat16 [32, 65536], P(('grp', 'node')), parts along dimension 0
The draws below stay inside these ranges and needn't reach their ends.
There are 2 independent parts, one for each index of `grp`. The reference program is written for one: setup_inputs(seed, part) draws one part's arguments, and reference() takes and returns one part's arrays. A program takes and returns all parts, laid end to end along the dimension named above; an argument that names none is the same for every part. Nothing has to cross between parts.
Inputs may be any that keep to these rules, and one draw needn't show every extreme that they name: `routes`: each token names 2 different replicas; within the rows of one device no replica is named by more than 4 tokens. `lengths`: some request has all 1280 positions filled.
All inputs are finite; a program needn't handle non-finite values.
Results may differ from the reference program's by a relative error of at most 0.0077.
Values may be sent and summed in bfloat16 or wider, within the bound.
No kernel may reach another device: no remote copies, remote signals or barrier semaphores. Data moves between devices by JAX's collectives and lax.ppermute only.
A program may use at most 128 MiB of HBM per device.

```python
import math
import jax
import jax.numpy as jnp
import numpy as np
from jax import lax

D = 7168
FF = 1024
SPLIT = 4
HEADS = 128
LATENT = 576
VALUE_DIM = 512
CACHE = 1280
TOK_DEV = 4
SLOTS = 4
TOP = 2
CAP = 4
TOKENS = 64
ATT_ROWS = 16
N_NODE = 16


def lengths_of(key):
    first_key, second_key = jax.random.split(jax.random.fold_in(key, 17))
    values = jax.random.randint(first_key, (ATT_ROWS,), 1, CACHE + 1)
    where_full = jax.random.randint(second_key, (), 0, ATT_ROWS)
    return (values.at[where_full].set(CACHE).astype(jnp.int32), where_full)


def cache_of(key):
    normal_rows = jax.random.normal(jax.random.fold_in(key, 29), (ATT_ROWS, CACHE, LATENT), jnp.float32)
    return jnp.clip(normal_rows, -6.0, 6.0)


def draw_lengths(key, part):
    return lengths_of(key)[0]


def draw_cache(key, part):
    return cache_of(key).astype(jnp.bfloat16)


def draw_queries(key, part):
    filled, where_full = lengths_of(key)
    stored = cache_of(key).astype(jnp.bfloat16).astype(jnp.float32)
    key_list = jax.random.split(jax.random.fold_in(key, 31), 8)
    drawn_rows = jnp.clip(jax.random.normal(key_list[0], (ATT_ROWS, HEADS, LATENT), jnp.float32), -6.0, 6.0)
    request_pick = jax.random.randint(key_list[1], (ATT_ROWS,), 0, 4) == 0
    request_pick = request_pick.at[where_full].set(True) & (filled >= 2)
    drawn_head = jax.random.randint(key_list[3], (ATT_ROWS, 1), 0, HEADS)
    head_pick = (jax.random.randint(key_list[2], (ATT_ROWS, HEADS), 0, 8) == 0) | (jnp.arange(HEADS, dtype=jnp.int32)[None, :] == drawn_head)
    chosen = request_pick[:, None] & head_pick
    first_pos = jax.random.randint(key_list[4], (ATT_ROWS,), 0, 1 << 30) % filled
    offset_pos = 1 + jax.random.randint(key_list[5], (ATT_ROWS,), 0, 1 << 30) % jnp.maximum(filled - 1, 1)
    second_pos = (first_pos + offset_pos) % filled
    request_ids = jnp.arange(ATT_ROWS, dtype=jnp.int32)
    key_one = stored[request_ids, first_pos]
    key_two = stored[request_ids, second_pos]
    norm_one = jnp.sum(key_one * key_one, axis=-1)[:, None]
    norm_two = jnp.sum(key_two * key_two, axis=-1)[:, None]
    cross_term = jnp.sum(key_one * key_two, axis=-1)[:, None]
    determinant = norm_one * norm_two - cross_term * cross_term
    strength_list = jnp.array([110.0, 230.0, 360.0], jnp.float32)
    strengths = strength_list[jax.random.randint(key_list[6], (ATT_ROWS, HEADS), 0, 3)]
    score_gap = jax.random.uniform(key_list[7], (ATT_ROWS, HEADS), jnp.float32, 1.0, 3.0)
    scale_root = 192.0 ** 0.5
    target_one = strengths * scale_root
    target_two = (strengths - score_gap) * scale_root
    weight_one = (target_one * norm_two - target_two * cross_term) / determinant
    weight_two = (target_two * norm_one - target_one * cross_term) / determinant
    aligned = weight_one[:, :, None] * key_one[:, None, :] + weight_two[:, :, None] * key_two[:, None, :]
    queries_out = jnp.where(chosen[:, :, None], jnp.clip(aligned, -60.0, 60.0), drawn_rows)
    return queries_out.astype(jnp.bfloat16)


def level_of(rng, dims, pieces, least, largest):
    def one(position, blocks):
        heights = jax.random.uniform(jax.random.fold_in(jax.random.fold_in(rng, 6), position), (blocks,), jnp.float32, least / len(pieces), largest / len(pieces))
        return jnp.repeat(jnp.exp(heights), dims[position] // blocks).reshape((-1,) + (1,) * (len(dims) - position - 1))

    loudness = one(*pieces[0])
    for cut in pieces[1:]:
        loudness = loudness * one(*cut)
    return loudness


def deal_out(rng, own, number, rows, amount, top, bound, slope):
    sequence = jax.random.permutation(rng, amount)
    crowded, common = shares(amount, rows * top, bound, slope, True), shares(amount, rows * top, bound, slope, False)
    places = jnp.arange(amount)

    def named(sizes, turn):
        used = int((sizes > 0).sum())
        fixed = max(1, used // 4)
        passed = fixed + (places - fixed + turn * (used - fixed)) % max(1, amount - fixed)
        return jnp.zeros((amount,), jnp.int32).at[sequence[jnp.where(places < fixed, places, passed)]].set(jnp.asarray(sizes, jnp.int32))

    sizes = jnp.where(number % 4 == 0, named(crowded, number // 4), named(common, number - number // 4 - 1))
    mixed = jax.random.permutation(jax.random.fold_in(own, 3), amount)
    giver, receiver = mixed[0:amount // 2 * 2:2], mixed[1:amount // 2 * 2:2]
    margin = jnp.minimum(sizes[giver] - 1, bound - sizes[receiver]) // 2
    margin = jnp.where((giver == sequence[0]) | (receiver == sequence[0]) | (sizes[receiver] == 0), 0, jnp.maximum(margin, 0))
    passed = jax.random.randint(jax.random.fold_in(own, 4), (amount // 2,), 0, 1 << 20) % (margin + 1)
    sizes = sizes.at[giver].add(-passed).at[receiver].add(passed)
    members = jnp.searchsorted(jnp.cumsum(sizes), jnp.arange(rows * top), side="right").astype(jnp.int32)
    grid = members.reshape(top, rows).T
    grid = grid[jax.random.permutation(jax.random.fold_in(own, 1), rows)]
    turn = jax.random.randint(jax.random.fold_in(own, 2), (rows, 1), 0, top)
    return jnp.take_along_axis(grid, (jnp.arange(top)[None, :] + turn) % top, axis=1)


def shares(amount, total, limit, slope, full):
    loads = [(1 << 20) // math.isqrt(grade ** slope) + 1 for grade in range(1, amount + 1)]
    largest = limit if full else min(limit, max(-(-total // amount), total * loads[0] // sum(loads)))
    least = 1 if total - largest >= amount - 1 else 0
    counts, surplus = [largest] + [least] * (amount - 1), total - largest - least * (amount - 1)
    while surplus > 0:
        candidates = [i for i in range(1, amount) if counts[i] < largest] or [i for i in range(1, amount) if counts[i] < limit]
        mass, left = sum([loads[i] for i in candidates]), surplus
        for i in candidates:
            addition = min(limit - counts[i], max(1, left * loads[i] // mass), surplus)
            counts[i] = counts[i] + addition
            surplus = surplus - addition
    return np.array(counts)


def centred(key, dims, width, most, cuts=(), kind=jnp.bfloat16):
    values = jax.random.normal(key, dims, jnp.float32) * width
    if len(cuts) > 0:
        values = level_of(key, dims, cuts, -0.22, 0.18) * values
    return jnp.clip(values, min=-most, max=most).astype(kind)


def setup_inputs(seed: int = 0, part: int = 0) -> dict:
    arg_keys = jax.random.split(jax.random.key(seed), 11)
    own_keys = jax.random.split(jax.random.fold_in(arg_keys[10], part), 11)
    tokens = centred(own_keys[0], (TOKENS, D), 1.0, 6.0, ((0, 16),))
    routes_keys = jax.random.split(jax.random.fold_in(own_keys[1], 1), TOKENS // TOK_DEV)
    routes_turns = jax.random.permutation(jax.random.fold_in(own_keys[1], 3), TOKENS // TOK_DEV)
    routes = jax.vmap(lambda own, number: deal_out(jax.random.fold_in(own_keys[1], 2), own, number, TOK_DEV, SLOTS, TOP, CAP, 2))(routes_keys, routes_turns).reshape((TOKENS, TOP))
    gates = jnp.clip(jnp.exp(math.log(1.0) - 2.9957323 * jax.random.uniform(own_keys[2], (TOKENS, TOP), jnp.float32) ** level_of(own_keys[2], (TOKENS, TOP), ((0, 16),), -0.2, 0.2)), 0.05, 1.0)
    norm_gain = jnp.clip(1.0 + 0.1 * jax.random.normal(arg_keys[3], (D,), jnp.float32), 0.5, 1.5).astype(jnp.bfloat16)
    w_gate = centred(arg_keys[4], (SLOTS * SPLIT, D, FF // SPLIT), D ** -0.5, 0.0625, ((0, 16),))
    w_up = centred(arg_keys[5], (SLOTS * SPLIT, D, FF // SPLIT), D ** -0.5, 0.0625, ((0, 16),))
    w_down = centred(arg_keys[6], (SLOTS * SPLIT, FF // SPLIT, D), FF ** -0.5, 0.1875, ((0, 16),))
    queries = draw_queries(jax.random.fold_in(jax.random.fold_in(arg_keys[10], part), 71), part)
    cache = draw_cache(jax.random.fold_in(jax.random.fold_in(arg_keys[10], part), 71), part)
    lengths = draw_lengths(jax.random.fold_in(jax.random.fold_in(arg_keys[10], part), 71), part)
    return dict(tokens=tokens, routes=routes, gates=gates, norm_gain=norm_gain, w_gate=w_gate, w_up=w_up, w_down=w_down, queries=queries, cache=cache, lengths=lengths)


norm_eps = 1e-06
route_scale = 2.5
softmax_scale = 192.0 ** (-0.5)

def reference(tokens, routes, gates, norm_gain, w_gate, w_up, w_down, queries, cache, lengths):
    hidden_in = tokens.astype(jnp.float32)
    inverse = lax.rsqrt(lax.optimization_barrier(jnp.mean(hidden_in * hidden_in, axis=-1, keepdims=True)) + norm_eps)
    normed = (hidden_in * inverse * norm_gain.astype(jnp.float32)).astype(jnp.bfloat16)
    mixing = route_scale * gates / lax.optimization_barrier(jnp.sum(gates, axis=-1, keepdims=True))
    flat_routes = routes.reshape(-1)
    flat_mixing = mixing.reshape(-1)
    most_rows = N_NODE * CAP

    def one_slot(total, slot_id):
        hits = flat_routes == slot_id
        found = jnp.nonzero(hits, size=most_rows, fill_value=0)[0].astype(jnp.int32)
        valid = jnp.arange(most_rows, dtype=jnp.int32) < jnp.sum(hits.astype(jnp.int32))
        row_ids = found // TOP
        chosen = normed[row_ids]
        summed = jnp.zeros((most_rows, D), jnp.float32)
        for piece in range(SPLIT):
            index = slot_id * SPLIT + piece
            gate_part = jnp.dot(chosen, w_gate[index], preferred_element_type=jnp.float32)
            up_part = jnp.dot(chosen, w_up[index], preferred_element_type=jnp.float32)
            hidden = (jax.nn.silu(gate_part) * up_part).astype(jnp.bfloat16)
            result = jnp.dot(hidden, w_down[index], preferred_element_type=jnp.float32).astype(jnp.bfloat16)
            summed = summed + result.astype(jnp.float32)
        summed_round = lax.optimization_barrier(summed.astype(jnp.bfloat16)).astype(jnp.float32)
        weighted = summed_round * flat_mixing[found][:, None]
        target = jnp.where(valid, row_ids, TOKENS)
        return (total.at[target].add(weighted.astype(total.dtype), mode='drop'), None)
    start = jnp.zeros((TOKENS, D), jnp.float32)
    total, unused = lax.scan(one_slot, start, jnp.arange(SLOTS, dtype=jnp.int32))
    moe_out = total.astype(jnp.bfloat16)

    def one_request(packed):
        query_row, cache_row, filled = packed
        scores = jnp.einsum('hc,jc->hj', query_row.astype(jnp.float32), cache_row.astype(jnp.float32)) * softmax_scale
        valid = jnp.arange(CACHE, dtype=jnp.int32)[None, :] < filled
        scores = jnp.where(valid, scores, -jnp.inf)
        probs = jax.nn.softmax(scores, axis=-1).astype(jnp.bfloat16)
        attended = jnp.dot(probs, cache_row[:, :VALUE_DIM], preferred_element_type=jnp.float32)
        return attended.astype(jnp.bfloat16).reshape(HEADS * VALUE_DIM)
    attention_out = lax.map(one_request, (queries, cache, lengths))
    return (moe_out, attention_out)
```

```python
import jax
import jax.numpy as jnp
from jax import lax
from jax.sharding import PartitionSpec as P

SPLIT = 4
VALUE_DIM = 512
LANES = 128


norm_eps = 1e-06
route_scale = 2.5
softmax_scale = 192.0 ** (-0.5)


def exchange_steps(node_count):
    bits = [1 << bit for bit in range(node_count.bit_length() - 1)]
    far, near = bits[3:], bits[1:3]
    steps = [(mask, mask) for mask in reversed(far)]
    steps += [(even, odd) for even, odd in zip(near, reversed(near))]
    return steps + [(1, 1)]


def trade(value, masks, node_count):
    pairs = [(node, node ^ masks[node % 2]) for node in range(node_count)]
    return lax.ppermute(value, "node", pairs)


def attention(queries, cache, lengths):
    cache_len = cache.shape[1]
    scores = (
        jnp.einsum("rhc,rjc->rhj", queries, cache, preferred_element_type=jnp.float32)
        * softmax_scale
    )
    valid = jnp.arange(cache_len, dtype=jnp.int32)[None, None, :] < lengths[:, None, None]
    scores = jnp.where(valid, scores, -jnp.inf)
    probs = jax.nn.softmax(scores, axis=-1).astype(jnp.bfloat16)
    attended = jnp.einsum(
        "rhj,rjv->rhv", probs, cache[:, :, :VALUE_DIM], preferred_element_type=jnp.float32
    )
    return attended.astype(jnp.bfloat16).reshape(queries.shape[0], -1)


def per_device(tokens, routes, gates, norm_gain, w_gate, w_up, w_down, queries, cache, lengths):
    width = tokens.shape[1]
    picks = routes.shape[1]
    node_count = lax.axis_size("node")
    steps = exchange_steps(node_count)

    mixing = route_scale * gates / jnp.sum(gates, axis=-1, keepdims=True)
    high = lax.reduce_precision(mixing, 8, 7)
    notes = jnp.concatenate([routes.astype(jnp.float32), high, mixing - high], axis=1)
    notes = jnp.pad(notes, ((0, 0), (0, -(3 * picks) % LANES))).astype(jnp.bfloat16)
    rows = jnp.concatenate([tokens, notes], axis=1)
    for masks in steps:
        rows = jnp.concatenate([rows, trade(rows, masks, node_count)], axis=0)

    notes = rows[:, width : width + 3 * picks].astype(jnp.float32)
    replica = (lax.axis_index("node") // SPLIT).astype(jnp.float32)
    weight = notes[:, picks : 2 * picks] + notes[:, 2 * picks :]
    share = jnp.sum(jnp.where(notes[:, :picks] == replica, weight, 0.0), axis=1, keepdims=True)

    hidden_in = rows[:, :width].astype(jnp.float32)
    inverse = lax.rsqrt(jnp.mean(hidden_in * hidden_in, axis=-1, keepdims=True) + norm_eps)
    normed = (hidden_in * inverse * norm_gain.astype(jnp.float32)).astype(jnp.bfloat16)
    gate_part = jnp.dot(normed, w_gate[0], preferred_element_type=jnp.float32)
    up_part = jnp.dot(normed, w_up[0], preferred_element_type=jnp.float32)
    hidden = (jax.nn.silu(gate_part) * up_part * share).astype(jnp.bfloat16)
    total = jnp.dot(hidden, w_down[0], preferred_element_type=jnp.float32)

    for masks in reversed(steps):
        half = total.shape[0] // 2
        arrived = trade(total[half:].astype(jnp.bfloat16), masks, node_count)
        total = total[:half] + arrived.astype(jnp.float32)
    moe_out = total.astype(jnp.bfloat16)

    return (moe_out, attention(queries, cache, lengths))


def solution(mesh):
    in_specs = (
        P(("grp", "node"), None),
        P(("grp", "node"), None),
        P(("grp", "node"), None),
        P(),
        P("node", None, None),
        P("node", None, None),
        P("node", None, None),
        P(("grp", "node"), None, None),
        P(("grp", "node"), None, None),
        P(("grp", "node")),
    )
    out_specs = (P(("grp", "node"), None), P(("grp", "node"), None))
    return jax.shard_map(
        per_device, mesh=mesh, in_specs=in_specs, out_specs=out_specs, check_vma=False
    )
```

```python
import functools

import jax
import jax.numpy as jnp
from jax import lax
from jax.experimental import pallas as pl
from jax.experimental.pallas import tpu as pltpu
from jax.sharding import PartitionSpec as P

SPLIT = 4
CHUNK = 1024
VALUE_DIM = 512
LANES = 128
VMEM_LIMIT = 24 * 1024 * 1024


norm_eps = 1e-06
route_scale = 2.5
softmax_scale = 192.0 ** (-0.5)


def exchange_steps(node_count):
    nodes = range(node_count)
    far = [bit for bit in range(3, node_count.bit_length() - 1)]
    steps = [[node ^ (1 << bit) ^ (1 if bit == far[-1] else 0) for node in nodes] for bit in reversed(far)]
    for first, second in ((3, 5), (5, 3)):
        steps.append([node ^ (second if (node & 7).bit_count() % 2 else first) for node in nodes])
    return steps + [[node ^ 1 for node in nodes]]


def trade(value, partners):
    return lax.ppermute(value, "node", list(enumerate(partners)))


def in_hbm(array):
    return pltpu.with_memory_space_constraint(array, pltpu.HBM)


def pack_kernel(tokens_hbm, routes_hbm, gates_hbm, rows_ref, tokens_ref, routes_ref, gates_ref, sem):
    sources, targets = (routes_hbm, gates_hbm, tokens_hbm), (routes_ref, gates_ref, tokens_ref)
    copies = [
        pltpu.make_async_copy(source, target, sem.at[index])
        for index, (source, target) in enumerate(zip(sources, targets))
    ]
    for copy in copies:
        copy.start()
    count, width = tokens_ref.shape
    picks = routes_ref.shape[0]
    copies[0].wait()
    copies[1].wait()
    gates = gates_ref[...]
    mixing = route_scale * gates / jnp.sum(gates, axis=0, keepdims=True)
    high = mixing.astype(jnp.bfloat16).astype(jnp.float32)
    parts = [routes_ref[...].astype(jnp.float32), high, mixing - high]
    row = lax.broadcasted_iota(jnp.int32, (count, count), 0)
    diagonal = row == lax.broadcasted_iota(jnp.int32, (count, count), 1)
    lane = lax.broadcasted_iota(jnp.int32, (count, LANES), 1)
    notes = jnp.zeros((count, LANES), jnp.float32)
    for part, values in enumerate(parts):
        for pick in range(picks):
            spread = jnp.broadcast_to(values[pick : pick + 1], (count, count))
            column = jnp.sum(jnp.where(diagonal, spread, 0.0), axis=1, keepdims=True)
            notes = jnp.where(lane == part * picks + pick, column, notes)
    rows_ref[:, width:] = notes.astype(jnp.bfloat16)
    copies[2].wait()
    rows_ref[:, :width] = tokens_ref[...]


def pack(tokens, routes, gates):
    count, width = tokens.shape
    picks = routes.shape[1]
    hbm = pl.BlockSpec(memory_space=pltpu.HBM)
    return pl.pallas_call(
        pack_kernel,
        out_shape=jax.ShapeDtypeStruct((count, width + LANES), jnp.bfloat16),
        in_specs=[hbm, hbm, hbm],
        scratch_shapes=[
            pltpu.VMEM((count, width), jnp.bfloat16),
            pltpu.VMEM((picks, count), jnp.int32),
            pltpu.VMEM((picks, count), jnp.float32),
            pltpu.SemaphoreType.DMA((3,)),
        ],
        compiler_params=pltpu.CompilerParams(vmem_limit_bytes=VMEM_LIMIT),
        name="pack",
    )(*map(in_hbm, (tokens, routes.T, gates.T)))


def load_kernel(*refs):
    count = len(refs) // 2 - 1
    sources, targets, done_ref, sem = refs[1 : 1 + count], refs[1 + count : -2], refs[-2], refs[-1]
    copies = [
        pltpu.make_async_copy(source, target, sem.at[index])
        for index, (source, target) in enumerate(zip(sources, targets))
    ]
    for copy in copies:
        copy.start()
    for copy in copies:
        copy.wait()
    done_ref[...] = jnp.zeros(done_ref.shape, done_ref.dtype)


def load(after, arrays):
    anywhere = pl.BlockSpec(memory_space=pl.ANY)
    vmem = pl.BlockSpec(memory_space=pltpu.VMEM)
    hbm = pl.BlockSpec(memory_space=pltpu.HBM)
    return pl.pallas_call(
        load_kernel,
        out_shape=tuple(pltpu.VMEM(a.shape, a.dtype) for a in arrays)
        + (jax.ShapeDtypeStruct((8, LANES), jnp.float32),),
        in_specs=[anywhere] + [hbm] * len(arrays),
        out_specs=(vmem,) * (len(arrays) + 1),
        scratch_shapes=[pltpu.SemaphoreType.DMA((len(arrays),))],
        compiler_params=pltpu.CompilerParams(vmem_limit_bytes=VMEM_LIMIT),
        cost_estimate=pl.CostEstimate(
            flops=0, bytes_accessed=sum(a.size * a.dtype.itemsize for a in arrays), transcendentals=0
        ),
        name="load",
    )(after, *map(in_hbm, arrays))


def attention_kernel(after_ref, lengths_ref, queries_hbm, cache_hbm, attended_ref, queries_ref, cache_ref, sem):
    copies = [
        pltpu.make_async_copy(queries_hbm, queries_ref, sem.at[0]),
        pltpu.make_async_copy(cache_hbm, cache_ref, sem.at[1]),
    ]
    for copy in copies:
        copy.start()
    for copy in copies:
        copy.wait()
    queries = queries_ref[0].T
    cached = cache_ref[0]
    scores = jnp.dot(queries, cached, preferred_element_type=jnp.float32) * softmax_scale
    position = lax.broadcasted_iota(jnp.int32, scores.shape, 1)
    scores = jnp.where(position < lengths_ref[0], scores, -jnp.inf)
    powers = jnp.exp(scores - jnp.max(scores, axis=-1, keepdims=True))
    probs = (powers / jnp.sum(powers, axis=-1, keepdims=True)).astype(jnp.bfloat16)
    attended = lax.dot_general(
        probs,
        cached[:VALUE_DIM],
        (((1,), (1,)), ((), ())),
        preferred_element_type=jnp.float32,
    )
    attended_ref[0] = attended.astype(jnp.bfloat16)


def attention(after, lengths, queries, cache):
    heads = queries.shape[1]
    queries = jnp.swapaxes(queries, 1, 2)
    cache = jnp.swapaxes(cache, 1, 2)
    hbm = pl.BlockSpec(memory_space=pltpu.HBM)
    return pl.pallas_call(
        attention_kernel,
        out_shape=jax.ShapeDtypeStruct((1, heads, VALUE_DIM), jnp.bfloat16),
        in_specs=[pl.BlockSpec(memory_space=pl.ANY), pl.BlockSpec(memory_space=pltpu.SMEM), hbm, hbm],
        scratch_shapes=[
            pltpu.VMEM(queries.shape, queries.dtype),
            pltpu.VMEM(cache.shape, cache.dtype),
            pltpu.SemaphoreType.DMA((2,)),
        ],
        compiler_params=pltpu.CompilerParams(vmem_limit_bytes=VMEM_LIMIT),
        cost_estimate=pl.CostEstimate(flops=360_000_000, bytes_accessed=1_700_000, transcendentals=164_000),
        name="attention",
    )(after, lengths, *map(in_hbm, (queries, cache)))


def experts_kernel(picks, loaded_ref, own_ref, other_ref, gain_ref, gate_ref, up_ref, down_ref, sum_ref, send_ref):
    width = gate_ref.shape[1]
    half = own_ref.shape[0]
    count = 2 * half
    gate_part = jnp.zeros((count, gate_ref.shape[2]), jnp.float32)
    up_part = jnp.zeros((count, up_ref.shape[2]), jnp.float32)
    squares = jnp.zeros((count, LANES), jnp.float32)
    for start in range(0, width, CHUNK):
        chunk = pl.ds(start, min(CHUNK, width - start))
        rows = jnp.concatenate([own_ref[:, chunk], other_ref[:, chunk]], axis=0).astype(jnp.float32)
        scaled = []
        for lane in range(0, rows.shape[1], LANES):
            part = rows[:, lane : lane + LANES]
            squares = squares + part * part
            index = (start + lane) // LANES
            scaled.append((part * gain_ref[index : index + 1, :].astype(jnp.float32)).astype(jnp.bfloat16))
        scaled = jnp.concatenate(scaled, axis=1)
        gate_part += jnp.dot(scaled, gate_ref[0, chunk, :], preferred_element_type=jnp.float32)
        up_part += jnp.dot(scaled, up_ref[0, chunk, :], preferred_element_type=jnp.float32)
    inverse = lax.rsqrt(jnp.sum(squares, axis=-1, keepdims=True) / width + norm_eps)
    gate_part = gate_part * inverse
    up_part = up_part * inverse
    notes = jnp.concatenate([own_ref[:, width:], other_ref[:, width:]], axis=0).astype(jnp.float32)
    replica = (lax.axis_index("node") // SPLIT).astype(jnp.float32)
    share = jnp.zeros((count, 1), jnp.float32)
    for pick in range(picks):
        weight = notes[:, picks + pick : picks + pick + 1] + notes[:, 2 * picks + pick : 2 * picks + pick + 1]
        share = share + jnp.where(notes[:, pick : pick + 1] == replica, weight, 0.0)
    hidden = gate_part / (1.0 + jnp.exp(-gate_part)) * up_part * share
    hidden = hidden.astype(jnp.bfloat16)
    for start in range(0, width, CHUNK):
        chunk = pl.ds(start, min(CHUNK, width - start))
        part = jnp.dot(hidden, down_ref[0, :, chunk], preferred_element_type=jnp.float32)
        sum_ref[:, chunk] = part[:half]
        send_ref[:, chunk] = part[half:].astype(jnp.bfloat16)


def experts(loaded, own, other, picks, norm_gain, w_gate, w_up, w_down):
    half = own.shape[0]
    width = w_gate.shape[1]
    weights = [pltpu.with_memory_space_constraint(w, pltpu.VMEM) for w in (w_gate, w_up, w_down)]
    vmem = pl.BlockSpec(memory_space=pltpu.VMEM)
    return pl.pallas_call(
        functools.partial(experts_kernel, picks),
        out_shape=(
            jax.ShapeDtypeStruct((half, width), jnp.float32),
            jax.ShapeDtypeStruct((half, width), jnp.bfloat16),
        ),
        in_specs=[pl.BlockSpec(memory_space=pl.ANY)] + [vmem] * 6,
        out_specs=(vmem, vmem),
        compiler_params=pltpu.CompilerParams(vmem_limit_bytes=VMEM_LIMIT),
        name="experts",
    )(loaded, own, other, norm_gain.reshape(-1, LANES), *weights)


def per_device(tokens, routes, gates, norm_gain, w_gate, w_up, w_down, queries, cache, lengths):
    node_count = lax.axis_size("node")
    steps = exchange_steps(node_count)
    rows = pack(tokens, routes, gates)
    for partners in steps[:-2]:
        rows = jnp.concatenate([rows, trade(rows, partners)], axis=0)
    *weights, loaded = load(rows, (w_gate, w_up, w_down))
    arrived, loaded = lax.optimization_barrier((trade(rows, steps[-2]), loaded))
    rows = jnp.concatenate([rows, arrived], axis=0)
    other = trade(rows, steps[-1])

    total, send = experts(loaded, rows, other, routes.shape[1], norm_gain, *weights)
    total = total + trade(send, steps[-1]).astype(jnp.float32)
    attended = attention(total, lengths, queries, cache)
    for partners in reversed(steps[:-1]):
        half = total.shape[0] // 2
        arrived = trade(total[half:].astype(jnp.bfloat16), partners)
        if partners is steps[-2]:
            arrived, attended = lax.optimization_barrier((arrived, attended))
            attention_out = attended.reshape(1, -1)
        if partners is steps[-3]:
            arrived, attention_out = lax.optimization_barrier((arrived, attention_out))
        total = total[:half] + arrived.astype(jnp.float32)
    moe_out = total.astype(jnp.bfloat16)

    return (moe_out, attention_out)


def solution(mesh):
    in_specs = (
        P(("grp", "node"), None),
        P(("grp", "node"), None),
        P(("grp", "node"), None),
        P(),
        P("node", None, None),
        P("node", None, None),
        P("node", None, None),
        P(("grp", "node"), None, None),
        P(("grp", "node"), None, None),
        P(("grp", "node")),
    )
    out_specs = (P(("grp", "node"), None), P(("grp", "node"), None))
    return jax.shard_map(
        per_device, mesh=mesh, in_specs=in_specs, out_specs=out_specs, check_vma=False
    )
```

```python
import functools

import jax
import jax.numpy as jnp
from jax import lax
from jax.experimental import pallas as pl
from jax.experimental.pallas import tpu as pltpu
from jax.sharding import PartitionSpec as P

SPLIT = 4
CHUNK = 1024
LOADS = 4
VALUE_DIM = 512
LANES = 128
VMEM_LIMIT = 24 * 1024 * 1024


norm_eps = 1e-06
route_scale = 2.5
softmax_scale = 192.0 ** (-0.5)


def exchange_steps(node_count):
    nodes = range(node_count)
    far = [[node ^ (1 << bit) for node in nodes] for bit in reversed(range(3, node_count.bit_length() - 1))]
    near = [[node ^ masks[node % 2] for node in nodes] for masks in ((2, 4), (4, 2), (6, 6))]
    return far, near, [node ^ 1 for node in nodes]


def trade(value, partners):
    return lax.ppermute(value, "node", list(enumerate(partners)))


def in_hbm(array):
    return pltpu.with_memory_space_constraint(array, pltpu.HBM)


def pack_kernel(tokens_hbm, routes_hbm, gates_hbm, rows_ref, tokens_ref, routes_ref, gates_ref, sem):
    sources, targets = (routes_hbm, gates_hbm, tokens_hbm), (routes_ref, gates_ref, tokens_ref)
    copies = [
        pltpu.make_async_copy(source, target, sem.at[index])
        for index, (source, target) in enumerate(zip(sources, targets))
    ]
    for copy in copies:
        copy.start()
    count, width = tokens_ref.shape
    picks = routes_ref.shape[0]
    copies[0].wait()
    copies[1].wait()
    gates = gates_ref[...]
    mixing = route_scale * gates / jnp.sum(gates, axis=0, keepdims=True)
    high = mixing.astype(jnp.bfloat16).astype(jnp.float32)
    parts = [routes_ref[...].astype(jnp.float32), high, mixing - high]
    row = lax.broadcasted_iota(jnp.int32, (count, count), 0)
    diagonal = row == lax.broadcasted_iota(jnp.int32, (count, count), 1)
    lane = lax.broadcasted_iota(jnp.int32, (count, LANES), 1)
    notes = jnp.zeros((count, LANES), jnp.float32)
    for part, values in enumerate(parts):
        for pick in range(picks):
            spread = jnp.broadcast_to(values[pick : pick + 1], (count, count))
            column = jnp.sum(jnp.where(diagonal, spread, 0.0), axis=1, keepdims=True)
            notes = jnp.where(lane == part * picks + pick, column, notes)
    rows_ref[:, width:] = notes.astype(jnp.bfloat16)
    copies[2].wait()
    rows_ref[:, :width] = tokens_ref[...]


def pack(tokens, routes, gates):
    count, width = tokens.shape
    picks = routes.shape[1]
    hbm = pl.BlockSpec(memory_space=pltpu.HBM)
    return pl.pallas_call(
        pack_kernel,
        out_shape=jax.ShapeDtypeStruct((count, width + LANES), jnp.bfloat16),
        in_specs=[hbm, hbm, hbm],
        scratch_shapes=[
            pltpu.VMEM((count, width), jnp.bfloat16),
            pltpu.VMEM((picks, count), jnp.int32),
            pltpu.VMEM((picks, count), jnp.float32),
            pltpu.SemaphoreType.DMA((3,)),
        ],
        compiler_params=pltpu.CompilerParams(vmem_limit_bytes=VMEM_LIMIT),
        name="pack",
    )(*map(in_hbm, (tokens, routes.T, gates.T)))


def load_kernel(count, extra, *refs):
    sources, targets = refs[:count], refs[count + extra : -2]
    done_ref, sem = refs[-2:]
    copies = []
    for index, (source, target) in enumerate(zip(sources, targets)):
        step = source.shape[1] // LOADS
        for part in range(LOADS):
            block = pl.ds(part * step, step)
            copies.append(
                pltpu.make_async_copy(source.at[:, block], target.at[:, block], sem.at[index * LOADS + part])
            )
    for copy in copies:
        copy.start()
    for copy in copies:
        copy.wait()
    done_ref[...] = jnp.zeros(done_ref.shape, done_ref.dtype)


def load(after, arrays, *others):
    anywhere = pl.BlockSpec(memory_space=pl.ANY)
    vmem = pl.BlockSpec(memory_space=pltpu.VMEM)
    hbm = pl.BlockSpec(memory_space=pltpu.HBM)
    return pl.pallas_call(
        functools.partial(load_kernel, len(arrays), 1 + len(others)),
        out_shape=tuple(pltpu.VMEM(a.shape, a.dtype) for a in arrays)
        + (jax.ShapeDtypeStruct((8, LANES), jnp.float32),),
        in_specs=[hbm] * len(arrays) + [anywhere] * (1 + len(others)),
        out_specs=(vmem,) * (len(arrays) + 1),
        scratch_shapes=[pltpu.SemaphoreType.DMA((len(arrays) * LOADS,))],
        compiler_params=pltpu.CompilerParams(vmem_limit_bytes=VMEM_LIMIT),
        cost_estimate=pl.CostEstimate(
            flops=0, bytes_accessed=sum(a.size * a.dtype.itemsize for a in arrays), transcendentals=0
        ),
        name="load",
    )(*map(in_hbm, arrays), after, *others)


def attention_kernel(after_ref, lengths_ref, queries_hbm, cache_hbm, attended_ref, queries_ref, cache_ref, sem):
    copies = [
        pltpu.make_async_copy(queries_hbm, queries_ref, sem.at[0]),
        pltpu.make_async_copy(cache_hbm, cache_ref, sem.at[1]),
    ]
    for copy in copies:
        copy.start()
    for copy in copies:
        copy.wait()
    queries = queries_ref[0].T
    cached = cache_ref[0]
    scores = jnp.dot(queries, cached, preferred_element_type=jnp.float32) * softmax_scale
    position = lax.broadcasted_iota(jnp.int32, scores.shape, 1)
    scores = jnp.where(position < lengths_ref[0], scores, -jnp.inf)
    powers = jnp.exp(scores - jnp.max(scores, axis=-1, keepdims=True))
    probs = (powers / jnp.sum(powers, axis=-1, keepdims=True)).astype(jnp.bfloat16)
    attended = lax.dot_general(
        probs,
        cached[:VALUE_DIM],
        (((1,), (1,)), ((), ())),
        preferred_element_type=jnp.float32,
    )
    attended_ref[0] = attended.astype(jnp.bfloat16)


def attention(after, lengths, queries, cache):
    heads = queries.shape[1]
    queries = jnp.swapaxes(queries, 1, 2)
    cache = jnp.swapaxes(cache, 1, 2)
    hbm = pl.BlockSpec(memory_space=pltpu.HBM)
    return pl.pallas_call(
        attention_kernel,
        out_shape=jax.ShapeDtypeStruct((1, heads, VALUE_DIM), jnp.bfloat16),
        in_specs=[pl.BlockSpec(memory_space=pl.ANY), pl.BlockSpec(memory_space=pltpu.SMEM), hbm, hbm],
        scratch_shapes=[
            pltpu.VMEM(queries.shape, queries.dtype),
            pltpu.VMEM(cache.shape, cache.dtype),
            pltpu.SemaphoreType.DMA((2,)),
        ],
        compiler_params=pltpu.CompilerParams(vmem_limit_bytes=VMEM_LIMIT),
        cost_estimate=pl.CostEstimate(flops=360_000_000, bytes_accessed=1_700_000, transcendentals=164_000),
        name="attention",
    )(after, lengths, *map(in_hbm, (queries, cache)))


def experts_kernel(picks, count, loaded_ref, *refs):
    pieces, (gain_ref, gate_ref, up_ref, down_ref) = refs[:count], refs[count : count + 4]
    outputs = refs[count + 4 :]
    width = gate_ref.shape[1]
    rows = [piece.shape[0] for piece in pieces]
    total = sum(rows)
    gate_part = jnp.zeros((total, gate_ref.shape[2]), jnp.float32)
    up_part = jnp.zeros((total, up_ref.shape[2]), jnp.float32)
    squares = [jnp.zeros((size, LANES), jnp.float32) for size in rows]
    for start in range(0, width, CHUNK):
        stop = min(start + CHUNK, width)
        scaled = []
        for lane in range(start, stop, LANES):
            gain = gain_ref[lane // LANES : lane // LANES + 1, :].astype(jnp.float32)
            column = []
            for index, piece in enumerate(pieces):
                part = piece[:, lane : lane + LANES].astype(jnp.float32)
                squares[index] = squares[index] + part * part
                column.append(part * gain)
            scaled.append(jnp.concatenate(column, axis=0).astype(jnp.bfloat16))
        scaled = jnp.concatenate(scaled, axis=1)
        gate_part += jnp.dot(scaled, gate_ref[0, start:stop, :], preferred_element_type=jnp.float32)
        up_part += jnp.dot(scaled, up_ref[0, start:stop, :], preferred_element_type=jnp.float32)
    squares = jnp.concatenate(squares, axis=0)
    inverse = lax.rsqrt(jnp.sum(squares, axis=-1, keepdims=True) / width + norm_eps)
    gate_part = gate_part * inverse
    up_part = up_part * inverse
    notes = jnp.concatenate([piece[:, width:].astype(jnp.float32) for piece in pieces], axis=0)
    replica = (lax.axis_index("node") // SPLIT).astype(jnp.float32)
    share = jnp.zeros((total, 1), jnp.float32)
    for pick in range(picks):
        weight = notes[:, picks + pick : picks + pick + 1] + notes[:, 2 * picks + pick : 2 * picks + pick + 1]
        share = share + jnp.where(notes[:, pick : pick + 1] == replica, weight, 0.0)
    hidden = gate_part / (1.0 + jnp.exp(-gate_part)) * up_part * share
    hidden = hidden.astype(jnp.bfloat16)
    for start in range(0, width, CHUNK):
        stop = min(start + CHUNK, width)
        part = jnp.dot(hidden, down_ref[0, :, start:stop], preferred_element_type=jnp.float32)
        first = 0
        for size, output in zip(rows, outputs):
            output[:, start:stop] = part[first : first + size].astype(output.dtype)
            first += size


def experts(loaded, pieces, picks, gain, weights):
    count = len(pieces)
    width = weights[0].shape[1]
    types = [jnp.float32] * (count // 2) + [jnp.bfloat16] * (count - count // 2)
    vmem = pl.BlockSpec(memory_space=pltpu.VMEM)
    return pl.pallas_call(
        functools.partial(experts_kernel, picks, count),
        out_shape=tuple(
            jax.ShapeDtypeStruct((piece.shape[0], width), kind) for piece, kind in zip(pieces, types)
        ),
        in_specs=[pl.BlockSpec(memory_space=pl.ANY)] + [vmem] * (count + 4),
        out_specs=(vmem,) * count,
        compiler_params=pltpu.CompilerParams(vmem_limit_bytes=VMEM_LIMIT),
        name="experts",
    )(loaded, *pieces, gain, *(pltpu.with_memory_space_constraint(w, pltpu.VMEM) for w in weights))


def per_device(tokens, routes, gates, norm_gain, w_gate, w_up, w_down, queries, cache, lengths):
    far, near, core = exchange_steps(lax.axis_size("node"))
    gain = norm_gain.reshape(-1, LANES)

    rows = pack(tokens, routes, gates)
    gate, loaded = load(rows, (w_gate,))
    for partners in far:
        arrived, loaded = lax.optimization_barrier((trade(rows, partners), loaded))
        rows = jnp.concatenate([rows, arrived], axis=0)
    up, down, loaded = load(rows, (w_up, w_down), loaded)
    weights = (gate, up, down)
    pieces = [rows] + [trade(rows, partners) for partners in near]
    pieces[-1], loaded = lax.optimization_barrier((pieces[-1], loaded))
    pieces += [trade(piece, core) for piece in pieces]

    outputs = experts(loaded, pieces, routes.shape[1], gain, weights)
    own, other = outputs[:4], outputs[4:]
    sums = [mine + trade(theirs, core).astype(jnp.float32) for mine, theirs in zip(own[1:], other[1:])]
    attended = attention(sums[-1], lengths, queries, cache)
    backs = [trade(part.astype(jnp.bfloat16), partners) for part, partners in zip(sums, near)]
    total = own[0] + trade(other[0], core).astype(jnp.float32)
    backs[-1], attended = lax.optimization_barrier((backs[-1], attended))
    attention_out = attended.reshape(1, -1)
    for back in backs:
        total = total + back.astype(jnp.float32)
    for partners in reversed(far):
        half = total.shape[0] // 2
        arrived = trade(total[half:].astype(jnp.bfloat16), partners)
        arrived, attention_out = lax.optimization_barrier((arrived, attention_out))
        total = total[:half] + arrived.astype(jnp.float32)
    moe_out = total.astype(jnp.bfloat16)

    return (moe_out, attention_out)


def solution(mesh):
    in_specs = (
        P(("grp", "node"), None),
        P(("grp", "node"), None),
        P(("grp", "node"), None),
        P(),
        P("node", None, None),
        P("node", None, None),
        P("node", None, None),
        P(("grp", "node"), None, None),
        P(("grp", "node"), None, None),
        P(("grp", "node")),
    )
    out_specs = (P(("grp", "node"), None), P(("grp", "node"), None))
    return jax.shard_map(
        per_device, mesh=mesh, in_specs=in_specs, out_specs=out_specs, check_vma=False
    )
```

```python
import functools

import jax
import jax.numpy as jnp
from jax import lax
from jax.experimental import pallas as pl
from jax.experimental.pallas import tpu as pltpu
from jax.sharding import PartitionSpec as P

SPLIT = 4
CHUNK = 1024
VALUE_DIM = 512
LANES = 128
VMEM_LIMIT = 24 * 1024 * 1024


norm_eps = 1e-06
route_scale = 2.5
softmax_scale = 192.0 ** (-0.5)


def exchange_steps(node_count):
    nodes = range(node_count)
    far = [[node ^ (1 << bit) for node in nodes] for bit in reversed(range(3, node_count.bit_length() - 1))]
    near = [[node ^ masks[node % 2] for node in nodes] for masks in ((2, 4), (4, 2), (6, 6))]
    return far, near, [node ^ 1 for node in nodes]


def trade(value, partners):
    return lax.ppermute(value, "node", list(enumerate(partners)))


def in_hbm(array):
    return pltpu.with_memory_space_constraint(array, pltpu.HBM)


def pack_kernel(tokens_hbm, routes_hbm, gates_hbm, rows_ref, tokens_ref, routes_ref, gates_ref, sem):
    sources, targets = (routes_hbm, gates_hbm, tokens_hbm), (routes_ref, gates_ref, tokens_ref)
    copies = [
        pltpu.make_async_copy(source, target, sem.at[index])
        for index, (source, target) in enumerate(zip(sources, targets))
    ]
    for copy in copies:
        copy.start()
    count, width = tokens_ref.shape
    picks = routes_ref.shape[0]
    copies[0].wait()
    copies[1].wait()
    gates = gates_ref[...]
    mixing = route_scale * gates / jnp.sum(gates, axis=0, keepdims=True)
    high = mixing.astype(jnp.bfloat16).astype(jnp.float32)
    parts = [routes_ref[...].astype(jnp.float32), high, mixing - high]
    row = lax.broadcasted_iota(jnp.int32, (count, count), 0)
    diagonal = row == lax.broadcasted_iota(jnp.int32, (count, count), 1)
    lane = lax.broadcasted_iota(jnp.int32, (count, LANES), 1)
    notes = jnp.zeros((count, LANES), jnp.float32)
    for part, values in enumerate(parts):
        for pick in range(picks):
            spread = jnp.broadcast_to(values[pick : pick + 1], (count, count))
            column = jnp.sum(jnp.where(diagonal, spread, 0.0), axis=1, keepdims=True)
            notes = jnp.where(lane == part * picks + pick, column, notes)
    rows_ref[:, width:] = notes.astype(jnp.bfloat16)
    copies[2].wait()
    rows_ref[:, :width] = tokens_ref[...]


def pack(tokens, routes, gates):
    count, width = tokens.shape
    picks = routes.shape[1]
    hbm = pl.BlockSpec(memory_space=pltpu.HBM)
    return pl.pallas_call(
        pack_kernel,
        out_shape=jax.ShapeDtypeStruct((count, width + LANES), jnp.bfloat16),
        in_specs=[hbm, hbm, hbm],
        scratch_shapes=[
            pltpu.VMEM((count, width), jnp.bfloat16),
            pltpu.VMEM((picks, count), jnp.int32),
            pltpu.VMEM((picks, count), jnp.float32),
            pltpu.SemaphoreType.DMA((3,)),
        ],
        compiler_params=pltpu.CompilerParams(vmem_limit_bytes=VMEM_LIMIT),
        name="pack",
    )(*map(in_hbm, (tokens, routes.T, gates.T)))


def attention_kernel(after_ref, lengths_ref, queries_hbm, cache_hbm, attended_ref, queries_ref, cache_ref, sem):
    copies = [
        pltpu.make_async_copy(queries_hbm, queries_ref, sem.at[0]),
        pltpu.make_async_copy(cache_hbm, cache_ref, sem.at[1]),
    ]
    for copy in copies:
        copy.start()
    for copy in copies:
        copy.wait()
    queries = queries_ref[0].T
    cached = cache_ref[0]
    scores = jnp.dot(queries, cached, preferred_element_type=jnp.float32) * softmax_scale
    position = lax.broadcasted_iota(jnp.int32, scores.shape, 1)
    scores = jnp.where(position < lengths_ref[0], scores, -jnp.inf)
    powers = jnp.exp(scores - jnp.max(scores, axis=-1, keepdims=True))
    probs = (powers / jnp.sum(powers, axis=-1, keepdims=True)).astype(jnp.bfloat16)
    attended = lax.dot_general(
        probs,
        cached[:VALUE_DIM],
        (((1,), (1,)), ((), ())),
        preferred_element_type=jnp.float32,
    )
    attended_ref[0] = attended.astype(jnp.bfloat16)


def attention(after, lengths, queries, cache):
    heads = queries.shape[1]
    queries = jnp.swapaxes(queries, 1, 2)
    cache = jnp.swapaxes(cache, 1, 2)
    hbm = pl.BlockSpec(memory_space=pltpu.HBM)
    return pl.pallas_call(
        attention_kernel,
        out_shape=jax.ShapeDtypeStruct((1, heads, VALUE_DIM), jnp.bfloat16),
        in_specs=[pl.BlockSpec(memory_space=pl.ANY), pl.BlockSpec(memory_space=pltpu.SMEM), hbm, hbm],
        scratch_shapes=[
            pltpu.VMEM(queries.shape, queries.dtype),
            pltpu.VMEM(cache.shape, cache.dtype),
            pltpu.SemaphoreType.DMA((2,)),
        ],
        compiler_params=pltpu.CompilerParams(vmem_limit_bytes=VMEM_LIMIT),
        cost_estimate=pl.CostEstimate(flops=4_000_000_000, bytes_accessed=1_700_000, transcendentals=164_000),
        name="attention",
    )(after, lengths, *map(in_hbm, (queries, cache)))


def experts_kernel(picks, count, loaded_ref, *refs):
    pieces, (gain_ref, gate_ref, up_ref, down_ref) = refs[:count], refs[count : count + 4]
    outputs = refs[count + 4 :]
    width = gate_ref.shape[1]
    rows = [piece.shape[0] for piece in pieces]
    total = sum(rows)
    padding = -total % LANES
    gate_part = jnp.zeros((total + padding, gate_ref.shape[2]), jnp.float32)
    up_part = jnp.zeros((total + padding, up_ref.shape[2]), jnp.float32)
    squares = [jnp.zeros((size, LANES), jnp.float32) for size in rows]
    for start in range(0, width, CHUNK):
        stop = min(start + CHUNK, width)
        scaled = []
        for lane in range(start, stop, LANES):
            gain = gain_ref[lane // LANES : lane // LANES + 1, :].astype(jnp.float32)
            column = []
            for index, piece in enumerate(pieces):
                part = piece[:, lane : lane + LANES].astype(jnp.float32)
                squares[index] = squares[index] + part * part
                column.append(part * gain)
            if padding:
                column.append(jnp.zeros((padding, LANES), jnp.float32))
            scaled.append(jnp.concatenate(column, axis=0).astype(jnp.bfloat16))
        scaled = jnp.concatenate(scaled, axis=1)
        gate_part += jnp.dot(scaled, gate_ref[0, start:stop, :], preferred_element_type=jnp.float32)
        up_part += jnp.dot(scaled, up_ref[0, start:stop, :], preferred_element_type=jnp.float32)
    squares = jnp.concatenate(squares, axis=0)
    inverse = lax.rsqrt(jnp.sum(squares, axis=-1, keepdims=True) / width + norm_eps)
    gate_part = gate_part[:total] * inverse
    up_part = up_part[:total] * inverse
    notes = jnp.concatenate([piece[:, width:].astype(jnp.float32) for piece in pieces], axis=0)
    replica = (lax.axis_index("node") // SPLIT).astype(jnp.float32)
    share = jnp.zeros((total, 1), jnp.float32)
    for pick in range(picks):
        weight = notes[:, picks + pick : picks + pick + 1] + notes[:, 2 * picks + pick : 2 * picks + pick + 1]
        share = share + jnp.where(notes[:, pick : pick + 1] == replica, weight, 0.0)
    hidden = gate_part / (1.0 + jnp.exp(-gate_part)) * up_part * share
    hidden = hidden.astype(jnp.bfloat16)
    if padding:
        hidden = jnp.concatenate([hidden, jnp.zeros((padding, hidden.shape[1]), hidden.dtype)], axis=0)
    for start in range(0, width, CHUNK):
        stop = min(start + CHUNK, width)
        part = jnp.dot(hidden, down_ref[0, :, start:stop], preferred_element_type=jnp.float32)
        first = 0
        for size, output in zip(rows, outputs):
            output[:, start:stop] = part[first : first + size].astype(output.dtype)
            first += size


def experts(loaded, pieces, picks, gain, weights):
    count = len(pieces)
    width = weights[0].shape[1]
    types = [jnp.float32] * (count // 2) + [jnp.bfloat16] * (count - count // 2)
    vmem = pl.BlockSpec(memory_space=pltpu.VMEM)
    return pl.pallas_call(
        functools.partial(experts_kernel, picks, count),
        out_shape=tuple(
            jax.ShapeDtypeStruct((piece.shape[0], width), kind) for piece, kind in zip(pieces, types)
        ),
        in_specs=[pl.BlockSpec(memory_space=pl.ANY)] + [vmem] * (count + 4),
        out_specs=(vmem,) * count,
        compiler_params=pltpu.CompilerParams(vmem_limit_bytes=VMEM_LIMIT),
        name="experts",
    )(loaded, *pieces, gain, *weights)


def per_device(tokens, routes, gates, norm_gain, w_gate, w_up, w_down, queries, cache, lengths):
    far, near, core = exchange_steps(lax.axis_size("node"))
    gain = norm_gain.reshape(-1, LANES)

    rows = pack(tokens, routes, gates)
    for partners in far:
        rows = jnp.concatenate([rows, trade(rows, partners)], axis=0)
    attended = attention(rows, lengths, queries, cache)
    weights = (w_gate, w_up, w_down)
    pieces = [rows] + [trade(rows, partners) for partners in near]
    pieces[-1], attended = lax.optimization_barrier((pieces[-1], attended))
    pieces += [trade(piece, core) for piece in pieces]

    outputs = experts(attended, pieces, routes.shape[1], gain, weights)
    own, other = outputs[:4], outputs[4:]
    sums = [mine + trade(theirs, core).astype(jnp.float32) for mine, theirs in zip(own[1:], other[1:])]
    half = rows.shape[0] // 2
    backs = [trade(part.astype(jnp.bfloat16), partners) for part, partners in zip(sums[:2], near[:2])]
    both = sums[2].astype(jnp.bfloat16)
    back_far = trade(both[half:], near[2])
    back_near = trade(both[:half], near[2])
    total = own[0] + trade(other[0], core).astype(jnp.float32)
    attention_out = attended.reshape(1, -1)
    back_far, attention_out = lax.optimization_barrier((back_far, attention_out))
    for back in backs:
        total = total + back.astype(jnp.float32)
    send = (total[half:] + back_far.astype(jnp.float32)).astype(jnp.bfloat16)
    total = total[:half] + back_near.astype(jnp.float32)
    for index, partners in enumerate(reversed(far)):
        if index:
            half = total.shape[0] // 2
            send, total = total[half:].astype(jnp.bfloat16), total[:half]
        total = total + trade(send, partners).astype(jnp.float32)
    moe_out = total.astype(jnp.bfloat16)
    moe_out = total.astype(jnp.bfloat16)

    return (moe_out, attention_out)


def solution(mesh):
    in_specs = (
        P(("grp", "node"), None),
        P(("grp", "node"), None),
        P(("grp", "node"), None),
        P(),
        P("node", None, None),
        P("node", None, None),
        P("node", None, None),
        P(("grp", "node"), None, None),
        P(("grp", "node"), None, None),
        P(("grp", "node")),
    )
    out_specs = (P(("grp", "node"), None), P(("grp", "node"), None))
    return jax.shard_map(
        per_device, mesh=mesh, in_specs=in_specs, out_specs=out_specs, check_vma=False
    )
```

```python
import functools

import jax
import jax.numpy as jnp
from jax import lax
from jax.experimental import pallas as pl
from jax.experimental.pallas import tpu as pltpu
from jax.sharding import PartitionSpec as P

SPLIT = 4
CHUNK = 1024
VALUE_DIM = 512
LANES = 128
VMEM_LIMIT = 24 * 1024 * 1024


norm_eps = 1e-06
route_scale = 2.5
softmax_scale = 192.0 ** (-0.5)


def exchange_steps(node_count):
    nodes = range(node_count)
    far = [[node ^ (1 << bit) for node in nodes] for bit in reversed(range(3, node_count.bit_length() - 1))]
    near = [[node ^ masks[node % 2] for node in nodes] for masks in ((2, 4), (4, 2), (6, 6))]
    return far, near, [node ^ 1 for node in nodes]


def trade(value, partners):
    return lax.ppermute(value, "node", list(enumerate(partners)))


def in_hbm(array):
    return pltpu.with_memory_space_constraint(array, pltpu.HBM)


def pack_kernel(tokens_hbm, routes_hbm, gates_hbm, rows_ref, tokens_ref, routes_ref, gates_ref, sem):
    sources, targets = (routes_hbm, gates_hbm, tokens_hbm), (routes_ref, gates_ref, tokens_ref)
    copies = [
        pltpu.make_async_copy(source, target, sem.at[index])
        for index, (source, target) in enumerate(zip(sources, targets))
    ]
    for copy in copies:
        copy.start()
    count, width = tokens_ref.shape
    picks = routes_ref.shape[0]
    copies[0].wait()
    copies[1].wait()
    gates = gates_ref[...]
    mixing = route_scale * gates / jnp.sum(gates, axis=0, keepdims=True)
    high = mixing.astype(jnp.bfloat16).astype(jnp.float32)
    parts = [routes_ref[...].astype(jnp.float32), high, mixing - high]
    row = lax.broadcasted_iota(jnp.int32, (count, count), 0)
    diagonal = row == lax.broadcasted_iota(jnp.int32, (count, count), 1)
    lane = lax.broadcasted_iota(jnp.int32, (count, LANES), 1)
    notes = jnp.zeros((count, LANES), jnp.float32)
    for part, values in enumerate(parts):
        for pick in range(picks):
            spread = jnp.broadcast_to(values[pick : pick + 1], (count, count))
            column = jnp.sum(jnp.where(diagonal, spread, 0.0), axis=1, keepdims=True)
            notes = jnp.where(lane == part * picks + pick, column, notes)
    rows_ref[:, width:] = notes.astype(jnp.bfloat16)
    copies[2].wait()
    rows_ref[:, :width] = tokens_ref[...]


def pack(tokens, routes, gates):
    count, width = tokens.shape
    picks = routes.shape[1]
    hbm = pl.BlockSpec(memory_space=pltpu.HBM)
    return pl.pallas_call(
        pack_kernel,
        out_shape=jax.ShapeDtypeStruct((count, width + LANES), jnp.bfloat16),
        in_specs=[hbm, hbm, hbm],
        scratch_shapes=[
            pltpu.VMEM((count, width), jnp.bfloat16),
            pltpu.VMEM((picks, count), jnp.int32),
            pltpu.VMEM((picks, count), jnp.float32),
            pltpu.SemaphoreType.DMA((3,)),
        ],
        compiler_params=pltpu.CompilerParams(vmem_limit_bytes=VMEM_LIMIT),
        name="pack",
    )(*map(in_hbm, (tokens, routes.T, gates.T)))


def attention_kernel(after_ref, lengths_ref, queries_hbm, cache_hbm, attended_ref, queries_ref, cache_ref, sem):
    copies = [
        pltpu.make_async_copy(queries_hbm, queries_ref, sem.at[0]),
        pltpu.make_async_copy(cache_hbm, cache_ref, sem.at[1]),
    ]
    for copy in copies:
        copy.start()
    for copy in copies:
        copy.wait()
    queries = queries_ref[0].T
    cached = cache_ref[0]
    scores = jnp.dot(queries, cached, preferred_element_type=jnp.float32) * softmax_scale
    position = lax.broadcasted_iota(jnp.int32, scores.shape, 1)
    scores = jnp.where(position < lengths_ref[0], scores, -jnp.inf)
    powers = jnp.exp(scores - jnp.max(scores, axis=-1, keepdims=True))
    probs = (powers / jnp.sum(powers, axis=-1, keepdims=True)).astype(jnp.bfloat16)
    attended = lax.dot_general(
        probs,
        cached[:VALUE_DIM],
        (((1,), (1,)), ((), ())),
        preferred_element_type=jnp.float32,
    )
    attended_ref[0] = attended.astype(jnp.bfloat16)


def attention(after, lengths, queries, cache):
    heads = queries.shape[1]
    queries = jnp.swapaxes(queries, 1, 2)
    cache = jnp.swapaxes(cache, 1, 2)
    hbm = pl.BlockSpec(memory_space=pltpu.HBM)
    return pl.pallas_call(
        attention_kernel,
        out_shape=jax.ShapeDtypeStruct((1, heads, VALUE_DIM), jnp.bfloat16),
        in_specs=[pl.BlockSpec(memory_space=pl.ANY), pl.BlockSpec(memory_space=pltpu.SMEM), hbm, hbm],
        scratch_shapes=[
            pltpu.VMEM(queries.shape, queries.dtype),
            pltpu.VMEM(cache.shape, cache.dtype),
            pltpu.SemaphoreType.DMA((2,)),
        ],
        compiler_params=pltpu.CompilerParams(vmem_limit_bytes=VMEM_LIMIT),
        cost_estimate=pl.CostEstimate(flops=4_000_000_000, bytes_accessed=1_700_000, transcendentals=164_000),
        name="attention",
    )(after, lengths, *map(in_hbm, (queries, cache)))


def experts_kernel(picks, count, loaded_ref, *refs):
    pieces, (gain_ref, gate_ref, up_ref, down_ref) = refs[:count], refs[count : count + 4]
    outputs = refs[count + 4 :]
    width = gate_ref.shape[1]
    rows = [piece.shape[0] for piece in pieces]
    total = sum(rows)
    padding = -total % LANES
    gate_part = jnp.zeros((total + padding, gate_ref.shape[2]), jnp.float32)
    up_part = jnp.zeros((total + padding, up_ref.shape[2]), jnp.float32)
    squares = [jnp.zeros((size, LANES), jnp.float32) for size in rows]
    for start in range(0, width, CHUNK):
        stop = min(start + CHUNK, width)
        scaled = []
        for lane in range(start, stop, LANES):
            gain = gain_ref[lane // LANES : lane // LANES + 1, :].astype(jnp.float32)
            column = []
            for index, piece in enumerate(pieces):
                part = piece[:, lane : lane + LANES].astype(jnp.float32)
                squares[index] = squares[index] + part * part
                column.append(part * gain)
            if padding:
                column.append(jnp.zeros((padding, LANES), jnp.float32))
            scaled.append(jnp.concatenate(column, axis=0).astype(jnp.bfloat16))
        scaled = jnp.concatenate(scaled, axis=1)
        gate_part += jnp.dot(scaled, gate_ref[0, start:stop, :], preferred_element_type=jnp.float32)
        up_part += jnp.dot(scaled, up_ref[0, start:stop, :], preferred_element_type=jnp.float32)
    squares = jnp.concatenate(squares, axis=0)
    inverse = lax.rsqrt(jnp.sum(squares, axis=-1, keepdims=True) / width + norm_eps)
    gate_part = gate_part[:total] * inverse
    up_part = up_part[:total] * inverse
    notes = jnp.concatenate([piece[:, width:].astype(jnp.float32) for piece in pieces], axis=0)
    replica = (lax.axis_index("node") // SPLIT).astype(jnp.float32)
    share = jnp.zeros((total, 1), jnp.float32)
    for pick in range(picks):
        weight = notes[:, picks + pick : picks + pick + 1] + notes[:, 2 * picks + pick : 2 * picks + pick + 1]
        share = share + jnp.where(notes[:, pick : pick + 1] == replica, weight, 0.0)
    hidden = gate_part / (1.0 + jnp.exp(-gate_part)) * up_part * share
    hidden = hidden.astype(jnp.bfloat16)
    if padding:
        hidden = jnp.concatenate([hidden, jnp.zeros((padding, hidden.shape[1]), hidden.dtype)], axis=0)
    for start in range(0, width, CHUNK):
        stop = min(start + CHUNK, width)
        part = jnp.dot(hidden, down_ref[0, :, start:stop], preferred_element_type=jnp.float32)
        first = 0
        for size, output in zip(rows, outputs):
            output[:, start:stop] = part[first : first + size].astype(output.dtype)
            first += size


def experts(loaded, pieces, picks, gain, weights):
    count = len(pieces)
    width = weights[0].shape[1]
    types = [jnp.float32] * (count // 2) + [jnp.bfloat16] * (count - count // 2)
    vmem = pl.BlockSpec(memory_space=pltpu.VMEM)
    return pl.pallas_call(
        functools.partial(experts_kernel, picks, count),
        out_shape=tuple(
            jax.ShapeDtypeStruct((piece.shape[0], width), kind) for piece, kind in zip(pieces, types)
        ),
        in_specs=[pl.BlockSpec(memory_space=pl.ANY)] + [vmem] * (count + 4),
        out_specs=(vmem,) * count,
        compiler_params=pltpu.CompilerParams(vmem_limit_bytes=VMEM_LIMIT),
        name="experts",
    )(loaded, *pieces, gain, *weights)


def per_device(tokens, routes, gates, norm_gain, w_gate, w_up, w_down, queries, cache, lengths):
    far, near, core = exchange_steps(lax.axis_size("node"))
    gain = norm_gain.reshape(-1, LANES)

    rows = pack(tokens, routes, gates)
    for partners in far[:-1]:
        rows = jnp.concatenate([rows, trade(rows, partners)], axis=0)
    arrived = trade(rows, far[-1])
    diagonal = trade(rows, near[2])
    rows = jnp.concatenate([rows, arrived], axis=0)
    attended = attention(rows, lengths, queries, cache)
    weights = (w_gate, w_up, w_down)
    pieces = [rows] + [trade(rows, partners) for partners in near[:2]]
    pieces[1], attended = lax.optimization_barrier((pieces[1], attended))
    pieces.append(jnp.concatenate([diagonal, trade(arrived, near[2])], axis=0))
    pieces += [trade(piece, core) for piece in pieces]

    outputs = experts(attended, pieces, routes.shape[1], gain, weights)
    own, other = outputs[:4], outputs[4:]
    sums = [mine + trade(theirs, core).astype(jnp.float32) for mine, theirs in zip(own[1:], other[1:])]
    half = rows.shape[0] // 2
    backs = [trade(part.astype(jnp.bfloat16), partners) for part, partners in zip(sums[:2], near[:2])]
    both = sums[2].astype(jnp.bfloat16)
    back_far = trade(both[half:], near[2])
    back_near = trade(both[:half], near[2])
    total = own[0] + trade(other[0], core).astype(jnp.float32)
    attention_out = attended.reshape(1, -1)
    back_far, attention_out = lax.optimization_barrier((back_far, attention_out))
    for back in backs:
        total = total + back.astype(jnp.float32)
    send = (total[half:] + back_far.astype(jnp.float32)).astype(jnp.bfloat16)
    total = total[:half] + back_near.astype(jnp.float32)
    for index, partners in enumerate(reversed(far)):
        if index:
            half = total.shape[0] // 2
            send, total = total[half:].astype(jnp.bfloat16), total[:half]
        total = total + trade(send, partners).astype(jnp.float32)
    moe_out = total.astype(jnp.bfloat16)
    moe_out = total.astype(jnp.bfloat16)

    return (moe_out, attention_out)


def solution(mesh):
    in_specs = (
        P(("grp", "node"), None),
        P(("grp", "node"), None),
        P(("grp", "node"), None),
        P(),
        P("node", None, None),
        P("node", None, None),
        P("node", None, None),
        P(("grp", "node"), None, None),
        P(("grp", "node"), None, None),
        P(("grp", "node")),
    )
    out_specs = (P(("grp", "node"), None), P(("grp", "node"), None))
    return jax.shard_map(
        per_device, mesh=mesh, in_specs=in_specs, out_specs=out_specs, check_vma=False
    )
```

```python
import functools

import jax
import jax.numpy as jnp
from jax import lax
from jax.experimental import pallas as pl
from jax.experimental.pallas import tpu as pltpu
from jax.sharding import PartitionSpec as P

SPLIT = 4
CHUNK = 1024
VALUE_DIM = 512
LANES = 128
VMEM_LIMIT = 24 * 1024 * 1024


norm_eps = 1e-06
route_scale = 2.5
softmax_scale = 192.0 ** (-0.5)


def exchange_steps(node_count):
    nodes = range(node_count)
    far = [[node ^ (1 << bit) for node in nodes] for bit in reversed(range(3, node_count.bit_length() - 1))]
    near = [[node ^ masks[node % 2] for node in nodes] for masks in ((2, 4), (4, 2), (6, 6))]
    return far, near, [node ^ 1 for node in nodes]


def trade(value, partners):
    return lax.ppermute(value, "node", list(enumerate(partners)))


def in_hbm(array):
    return pltpu.with_memory_space_constraint(array, pltpu.HBM)


def pack_kernel(tokens_hbm, routes_hbm, gates_hbm, rows_ref, tokens_ref, routes_ref, gates_ref, sem):
    sources, targets = (routes_hbm, gates_hbm, tokens_hbm), (routes_ref, gates_ref, tokens_ref)
    copies = [
        pltpu.make_async_copy(source, target, sem.at[index])
        for index, (source, target) in enumerate(zip(sources, targets))
    ]
    for copy in copies:
        copy.start()
    count, width = tokens_ref.shape
    picks = routes_ref.shape[0]
    copies[0].wait()
    copies[1].wait()
    gates = gates_ref[...]
    mixing = route_scale * gates / jnp.sum(gates, axis=0, keepdims=True)
    high = mixing.astype(jnp.bfloat16).astype(jnp.float32)
    parts = [routes_ref[...].astype(jnp.float32), high, mixing - high]
    row = lax.broadcasted_iota(jnp.int32, (count, count), 0)
    diagonal = row == lax.broadcasted_iota(jnp.int32, (count, count), 1)
    lane = lax.broadcasted_iota(jnp.int32, (count, LANES), 1)
    notes = jnp.zeros((count, LANES), jnp.float32)
    for part, values in enumerate(parts):
        for pick in range(picks):
            spread = jnp.broadcast_to(values[pick : pick + 1], (count, count))
            column = jnp.sum(jnp.where(diagonal, spread, 0.0), axis=1, keepdims=True)
            notes = jnp.where(lane == part * picks + pick, column, notes)
    rows_ref[:, width:] = notes.astype(jnp.bfloat16)
    copies[2].wait()
    rows_ref[:, :width] = tokens_ref[...]


def pack(tokens, routes, gates):
    count, width = tokens.shape
    picks = routes.shape[1]
    hbm = pl.BlockSpec(memory_space=pltpu.HBM)
    return pl.pallas_call(
        pack_kernel,
        out_shape=jax.ShapeDtypeStruct((count, width + LANES), jnp.bfloat16),
        in_specs=[hbm, hbm, hbm],
        scratch_shapes=[
            pltpu.VMEM((count, width), jnp.bfloat16),
            pltpu.VMEM((picks, count), jnp.int32),
            pltpu.VMEM((picks, count), jnp.float32),
            pltpu.SemaphoreType.DMA((3,)),
        ],
        compiler_params=pltpu.CompilerParams(vmem_limit_bytes=VMEM_LIMIT),
        name="pack",
    )(*map(in_hbm, (tokens, routes.T, gates.T)))


def join_kernel(upper_ref, lower_ref, rows_ref):
    half = upper_ref.shape[0]
    rows_ref[:half] = upper_ref[...]
    rows_ref[half:] = lower_ref[...]


def join(upper, lower):
    half, width = upper.shape
    return pl.pallas_call(
        join_kernel,
        out_shape=jax.ShapeDtypeStruct((2 * half, width), upper.dtype),
        compiler_params=pltpu.CompilerParams(vmem_limit_bytes=VMEM_LIMIT),
        cost_estimate=pl.CostEstimate(flops=4_000_000_000, bytes_accessed=500_000, transcendentals=0),
        name="join",
    )(upper, lower)


def attention_kernel(after_ref, lengths_ref, queries_hbm, cache_hbm, attended_ref, queries_ref, cache_ref, sem):
    copies = [
        pltpu.make_async_copy(queries_hbm, queries_ref, sem.at[0]),
        pltpu.make_async_copy(cache_hbm, cache_ref, sem.at[1]),
    ]
    for copy in copies:
        copy.start()
    for copy in copies:
        copy.wait()
    queries = queries_ref[0].T
    cached = cache_ref[0]
    scores = jnp.dot(queries, cached, preferred_element_type=jnp.float32) * softmax_scale
    position = lax.broadcasted_iota(jnp.int32, scores.shape, 1)
    scores = jnp.where(position < lengths_ref[0], scores, -jnp.inf)
    powers = jnp.exp(scores - jnp.max(scores, axis=-1, keepdims=True))
    probs = (powers / jnp.sum(powers, axis=-1, keepdims=True)).astype(jnp.bfloat16)
    attended = lax.dot_general(
        probs,
        cached[:VALUE_DIM],
        (((1,), (1,)), ((), ())),
        preferred_element_type=jnp.float32,
    )
    attended_ref[0] = attended.astype(jnp.bfloat16)


def attention(after, lengths, queries, cache):
    heads = queries.shape[1]
    queries = jnp.swapaxes(queries, 1, 2)
    cache = jnp.swapaxes(cache, 1, 2)
    hbm = pl.BlockSpec(memory_space=pltpu.HBM)
    return pl.pallas_call(
        attention_kernel,
        out_shape=jax.ShapeDtypeStruct((1, heads, VALUE_DIM), jnp.bfloat16),
        in_specs=[pl.BlockSpec(memory_space=pl.ANY), pl.BlockSpec(memory_space=pltpu.SMEM), hbm, hbm],
        scratch_shapes=[
            pltpu.VMEM(queries.shape, queries.dtype),
            pltpu.VMEM(cache.shape, cache.dtype),
            pltpu.SemaphoreType.DMA((2,)),
        ],
        compiler_params=pltpu.CompilerParams(vmem_limit_bytes=VMEM_LIMIT),
        cost_estimate=pl.CostEstimate(flops=360_000_000, bytes_accessed=1_700_000, transcendentals=164_000),
        name="attention",
    )(after, lengths, *map(in_hbm, (queries, cache)))


def experts_kernel(picks, count, loaded_ref, *refs):
    pieces, (gain_ref, gate_ref, up_ref, down_ref) = refs[:count], refs[count : count + 4]
    outputs = refs[count + 4 :]
    width = gate_ref.shape[1]
    rows = [piece.shape[0] for piece in pieces]
    total = sum(rows)
    padding = -total % LANES
    gate_part = jnp.zeros((total + padding, gate_ref.shape[2]), jnp.float32)
    up_part = jnp.zeros((total + padding, up_ref.shape[2]), jnp.float32)
    squares = [jnp.zeros((size, LANES), jnp.float32) for size in rows]
    for start in range(0, width, CHUNK):
        stop = min(start + CHUNK, width)
        scaled = []
        for lane in range(start, stop, LANES):
            gain = gain_ref[lane // LANES : lane // LANES + 1, :].astype(jnp.float32)
            column = []
            for index, piece in enumerate(pieces):
                part = piece[:, lane : lane + LANES].astype(jnp.float32)
                squares[index] = squares[index] + part * part
                column.append(part * gain)
            if padding:
                column.append(jnp.zeros((padding, LANES), jnp.float32))
            scaled.append(jnp.concatenate(column, axis=0).astype(jnp.bfloat16))
        scaled = jnp.concatenate(scaled, axis=1)
        gate_part += jnp.dot(scaled, gate_ref[0, start:stop, :], preferred_element_type=jnp.float32)
        up_part += jnp.dot(scaled, up_ref[0, start:stop, :], preferred_element_type=jnp.float32)
    squares = jnp.concatenate(squares, axis=0)
    inverse = lax.rsqrt(jnp.sum(squares, axis=-1, keepdims=True) / width + norm_eps)
    gate_part = gate_part[:total] * inverse
    up_part = up_part[:total] * inverse
    notes = jnp.concatenate([piece[:, width:].astype(jnp.float32) for piece in pieces], axis=0)
    replica = (lax.axis_index("node") // SPLIT).astype(jnp.float32)
    share = jnp.zeros((total, 1), jnp.float32)
    for pick in range(picks):
        weight = notes[:, picks + pick : picks + pick + 1] + notes[:, 2 * picks + pick : 2 * picks + pick + 1]
        share = share + jnp.where(notes[:, pick : pick + 1] == replica, weight, 0.0)
    hidden = gate_part / (1.0 + jnp.exp(-gate_part)) * up_part * share
    hidden = hidden.astype(jnp.bfloat16)
    if padding:
        hidden = jnp.concatenate([hidden, jnp.zeros((padding, hidden.shape[1]), hidden.dtype)], axis=0)
    for start in range(0, width, CHUNK):
        stop = min(start + CHUNK, width)
        part = jnp.dot(hidden, down_ref[0, :, start:stop], preferred_element_type=jnp.float32)
        first = 0
        for size, output in zip(rows, outputs):
            output[:, start:stop] = part[first : first + size].astype(output.dtype)
            first += size


def experts(loaded, pieces, picks, gain, weights):
    count = len(pieces)
    width = weights[0].shape[1]
    types = [jnp.float32] * (count // 2) + [jnp.bfloat16] * (count - count // 2)
    vmem = pl.BlockSpec(memory_space=pltpu.VMEM)
    return pl.pallas_call(
        functools.partial(experts_kernel, picks, count),
        out_shape=tuple(
            jax.ShapeDtypeStruct((piece.shape[0], width), kind) for piece, kind in zip(pieces, types)
        ),
        in_specs=[pl.BlockSpec(memory_space=pl.ANY)] + [vmem] * (count + 4),
        out_specs=(vmem,) * count,
        compiler_params=pltpu.CompilerParams(vmem_limit_bytes=VMEM_LIMIT),
        name="experts",
    )(loaded, *pieces, gain, *weights)


def per_device(tokens, routes, gates, norm_gain, w_gate, w_up, w_down, queries, cache, lengths):
    far, near, core = exchange_steps(lax.axis_size("node"))
    gain = norm_gain.reshape(-1, LANES)

    rows = pack(tokens, routes, gates)
    for partners in far[:-1]:
        rows = jnp.concatenate([rows, trade(rows, partners)], axis=0)
    arrived = trade(rows, far[-1])
    diagonal = trade(rows, near[2])
    rows = join(rows, arrived)
    attended = attention(rows, lengths, queries, cache)
    weights = (w_gate, w_up, w_down)
    pieces = [rows] + [trade(rows, partners) for partners in near[:2]]
    pieces[1], attended = lax.optimization_barrier((pieces[1], attended))
    pieces.append(jnp.concatenate([diagonal, trade(arrived, near[2])], axis=0))
    pieces += [trade(piece, core) for piece in pieces]

    outputs = experts(rows, pieces, routes.shape[1], gain, weights)
    own, other = outputs[:4], outputs[4:]
    sums = [mine + trade(theirs, core).astype(jnp.float32) for mine, theirs in zip(own[1:], other[1:])]
    half = rows.shape[0] // 2
    backs = [trade(part.astype(jnp.bfloat16), partners) for part, partners in zip(sums[:2], near[:2])]
    both = sums[2].astype(jnp.bfloat16)
    back_far = trade(both[half:], near[2])
    back_near = trade(both[:half], near[2])
    total = own[0] + trade(other[0], core).astype(jnp.float32)
    attention_out = attended.reshape(1, -1)
    back_far, attention_out = lax.optimization_barrier((back_far, attention_out))
    for back in backs:
        total = total + back.astype(jnp.float32)
    send = (total[half:] + back_far.astype(jnp.float32)).astype(jnp.bfloat16)
    total = total[:half] + back_near.astype(jnp.float32)
    for index, partners in enumerate(reversed(far)):
        if index:
            half = total.shape[0] // 2
            send, total = total[half:].astype(jnp.bfloat16), total[:half]
        total = total + trade(send, partners).astype(jnp.float32)
    moe_out = total.astype(jnp.bfloat16)
    moe_out = total.astype(jnp.bfloat16)

    return (moe_out, attention_out)


def solution(mesh):
    in_specs = (
        P(("grp", "node"), None),
        P(("grp", "node"), None),
        P(("grp", "node"), None),
        P(),
        P("node", None, None),
        P("node", None, None),
        P("node", None, None),
        P(("grp", "node"), None, None),
        P(("grp", "node"), None, None),
        P(("grp", "node")),
    )
    out_specs = (P(("grp", "node"), None), P(("grp", "node"), None))
    return jax.shard_map(
        per_device, mesh=mesh, in_specs=in_specs, out_specs=out_specs, check_vma=False
    )
```

```python
import functools

import jax
import jax.numpy as jnp
from jax import lax
from jax.experimental import pallas as pl
from jax.experimental.pallas import tpu as pltpu
from jax.sharding import PartitionSpec as P

SPLIT = 4
CHUNK = 1024
VALUE_DIM = 512
LANES = 128
VMEM_LIMIT = 24 * 1024 * 1024


norm_eps = 1e-06
route_scale = 2.5
softmax_scale = 192.0 ** (-0.5)


def exchange_steps(node_count):
    nodes = range(node_count)
    far = [[node ^ (1 << bit) for node in nodes] for bit in reversed(range(3, node_count.bit_length() - 1))]
    near = [[node ^ masks[node % 2] for node in nodes] for masks in ((2, 4), (4, 2), (6, 6))]
    return far, near, [node ^ 1 for node in nodes]


def trade(value, partners):
    return lax.ppermute(value, "node", list(enumerate(partners)))


def in_hbm(array):
    return pltpu.with_memory_space_constraint(array, pltpu.HBM)


def pack_kernel(tokens_hbm, routes_hbm, gates_hbm, rows_ref, tokens_ref, routes_ref, gates_ref, sem):
    sources, targets = (routes_hbm, gates_hbm, tokens_hbm), (routes_ref, gates_ref, tokens_ref)
    copies = [
        pltpu.make_async_copy(source, target, sem.at[index])
        for index, (source, target) in enumerate(zip(sources, targets))
    ]
    for copy in copies:
        copy.start()
    count, width = tokens_ref.shape
    picks = routes_ref.shape[0]
    copies[0].wait()
    copies[1].wait()
    gates = gates_ref[...]
    mixing = route_scale * gates / jnp.sum(gates, axis=0, keepdims=True)
    high = mixing.astype(jnp.bfloat16).astype(jnp.float32)
    parts = [routes_ref[...].astype(jnp.float32), high, mixing - high]
    row = lax.broadcasted_iota(jnp.int32, (count, count), 0)
    diagonal = row == lax.broadcasted_iota(jnp.int32, (count, count), 1)
    lane = lax.broadcasted_iota(jnp.int32, (count, LANES), 1)
    notes = jnp.zeros((count, LANES), jnp.float32)
    for part, values in enumerate(parts):
        for pick in range(picks):
            spread = jnp.broadcast_to(values[pick : pick + 1], (count, count))
            column = jnp.sum(jnp.where(diagonal, spread, 0.0), axis=1, keepdims=True)
            notes = jnp.where(lane == part * picks + pick, column, notes)
    rows_ref[:, width:] = notes.astype(jnp.bfloat16)
    copies[2].wait()
    rows_ref[:, :width] = tokens_ref[...]


def pack(tokens, routes, gates):
    count, width = tokens.shape
    picks = routes.shape[1]
    hbm = pl.BlockSpec(memory_space=pltpu.HBM)
    return pl.pallas_call(
        pack_kernel,
        out_shape=jax.ShapeDtypeStruct((count, width + LANES), jnp.bfloat16),
        in_specs=[hbm, hbm, hbm],
        scratch_shapes=[
            pltpu.VMEM((count, width), jnp.bfloat16),
            pltpu.VMEM((picks, count), jnp.int32),
            pltpu.VMEM((picks, count), jnp.float32),
            pltpu.SemaphoreType.DMA((3,)),
        ],
        compiler_params=pltpu.CompilerParams(vmem_limit_bytes=VMEM_LIMIT),
        name="pack",
    )(*map(in_hbm, (tokens, routes.T, gates.T)))


def join_kernel(upper_ref, lower_ref, rows_ref):
    half = upper_ref.shape[0]
    rows_ref[:half] = upper_ref[...]
    rows_ref[half:] = lower_ref[...]


def join(upper, lower):
    half, width = upper.shape
    return pl.pallas_call(
        join_kernel,
        out_shape=jax.ShapeDtypeStruct((2 * half, width), upper.dtype),
        compiler_params=pltpu.CompilerParams(vmem_limit_bytes=VMEM_LIMIT),
        cost_estimate=pl.CostEstimate(flops=4_000_000_000, bytes_accessed=500_000, transcendentals=0),
        name="join",
    )(upper, lower)


def attention_kernel(after_ref, lengths_ref, queries_hbm, cache_hbm, attended_ref, queries_ref, cache_ref, sem):
    copies = [
        pltpu.make_async_copy(queries_hbm, queries_ref, sem.at[0]),
        pltpu.make_async_copy(cache_hbm, cache_ref, sem.at[1]),
    ]
    for copy in copies:
        copy.start()
    for copy in copies:
        copy.wait()
    queries = queries_ref[0].T
    cached = cache_ref[0]
    scores = jnp.dot(queries, cached, preferred_element_type=jnp.float32) * softmax_scale
    position = lax.broadcasted_iota(jnp.int32, scores.shape, 1)
    scores = jnp.where(position < lengths_ref[0], scores, -jnp.inf)
    powers = jnp.exp(scores - jnp.max(scores, axis=-1, keepdims=True))
    probs = (powers / jnp.sum(powers, axis=-1, keepdims=True)).astype(jnp.bfloat16)
    attended = lax.dot_general(
        probs,
        cached[:VALUE_DIM],
        (((1,), (1,)), ((), ())),
        preferred_element_type=jnp.float32,
    )
    attended_ref[0] = attended.astype(jnp.bfloat16)


def attention(after, lengths, queries, cache):
    heads = queries.shape[1]
    queries = jnp.swapaxes(queries, 1, 2)
    cache = jnp.swapaxes(cache, 1, 2)
    hbm = pl.BlockSpec(memory_space=pltpu.HBM)
    return pl.pallas_call(
        attention_kernel,
        out_shape=jax.ShapeDtypeStruct((1, heads, VALUE_DIM), jnp.bfloat16),
        in_specs=[pl.BlockSpec(memory_space=pl.ANY), pl.BlockSpec(memory_space=pltpu.SMEM), hbm, hbm],
        scratch_shapes=[
            pltpu.VMEM(queries.shape, queries.dtype),
            pltpu.VMEM(cache.shape, cache.dtype),
            pltpu.SemaphoreType.DMA((2,)),
        ],
        compiler_params=pltpu.CompilerParams(vmem_limit_bytes=VMEM_LIMIT),
        cost_estimate=pl.CostEstimate(flops=360_000_000, bytes_accessed=1_700_000, transcendentals=164_000),
        name="attention",
    )(after, lengths, *map(in_hbm, (queries, cache)))


def experts_kernel(picks, count, loaded_ref, *refs):
    pieces, (gain_ref, gate_ref, up_ref, down_ref) = refs[:count], refs[count : count + 4]
    outputs = refs[count + 4 :]
    width = gate_ref.shape[1]
    rows = [piece.shape[0] for piece in pieces]
    total = sum(rows)
    padding = -total % LANES
    gate_part = jnp.zeros((total + padding, gate_ref.shape[2]), jnp.float32)
    up_part = jnp.zeros((total + padding, up_ref.shape[2]), jnp.float32)
    squares = [jnp.zeros((size, LANES), jnp.float32) for size in rows]
    for start in range(0, width, CHUNK):
        stop = min(start + CHUNK, width)
        scaled = []
        for lane in range(start, stop, LANES):
            gain = gain_ref[lane // LANES : lane // LANES + 1, :].astype(jnp.float32)
            column = []
            for index, piece in enumerate(pieces):
                part = piece[:, lane : lane + LANES].astype(jnp.float32)
                squares[index] = squares[index] + part * part
                column.append(part * gain)
            if padding:
                column.append(jnp.zeros((padding, LANES), jnp.float32))
            scaled.append(jnp.concatenate(column, axis=0).astype(jnp.bfloat16))
        scaled = jnp.concatenate(scaled, axis=1)
        gate_part += jnp.dot(scaled, gate_ref[0, start:stop, :], preferred_element_type=jnp.float32)
        up_part += jnp.dot(scaled, up_ref[0, start:stop, :], preferred_element_type=jnp.float32)
    squares = jnp.concatenate(squares, axis=0)
    inverse = lax.rsqrt(jnp.sum(squares, axis=-1, keepdims=True) / width + norm_eps)
    gate_part = gate_part[:total] * inverse
    up_part = up_part[:total] * inverse
    notes = jnp.concatenate([piece[:, width:].astype(jnp.float32) for piece in pieces], axis=0)
    replica = (lax.axis_index("node") // SPLIT).astype(jnp.float32)
    share = jnp.zeros((total, 1), jnp.float32)
    for pick in range(picks):
        weight = notes[:, picks + pick : picks + pick + 1] + notes[:, 2 * picks + pick : 2 * picks + pick + 1]
        share = share + jnp.where(notes[:, pick : pick + 1] == replica, weight, 0.0)
    hidden = gate_part / (1.0 + jnp.exp(-gate_part)) * up_part * share
    hidden = hidden.astype(jnp.bfloat16)
    if padding:
        hidden = jnp.concatenate([hidden, jnp.zeros((padding, hidden.shape[1]), hidden.dtype)], axis=0)
    for start in range(0, width, CHUNK):
        stop = min(start + CHUNK, width)
        part = jnp.dot(hidden, down_ref[0, :, start:stop], preferred_element_type=jnp.float32)
        first = 0
        for size, output in zip(rows, outputs):
            output[:, start:stop] = part[first : first + size].astype(output.dtype)
            first += size


def experts(loaded, pieces, picks, gain, weights):
    count = len(pieces)
    width = weights[0].shape[1]
    types = [jnp.float32] * (count // 2) + [jnp.bfloat16] * (count - count // 2)
    vmem = pl.BlockSpec(memory_space=pltpu.VMEM)
    return pl.pallas_call(
        functools.partial(experts_kernel, picks, count),
        out_shape=tuple(
            jax.ShapeDtypeStruct((piece.shape[0], width), kind) for piece, kind in zip(pieces, types)
        ),
        in_specs=[pl.BlockSpec(memory_space=pl.ANY)] + [vmem] * (count + 4),
        out_specs=(vmem,) * count,
        compiler_params=pltpu.CompilerParams(vmem_limit_bytes=VMEM_LIMIT),
        cost_estimate=pl.CostEstimate(flops=2_000_000_000, bytes_accessed=500_000, transcendentals=0),
        name="experts",
    )(loaded, *pieces, gain, *weights)


def per_device(tokens, routes, gates, norm_gain, w_gate, w_up, w_down, queries, cache, lengths):
    far, near, core = exchange_steps(lax.axis_size("node"))
    gain = norm_gain.reshape(-1, LANES)

    rows = pack(tokens, routes, gates)
    for partners in far[:-1]:
        rows = jnp.concatenate([rows, trade(rows, partners)], axis=0)
    arrived = trade(rows, far[-1])
    diagonal = trade(rows, near[2])
    rows = join(rows, arrived)
    attended = attention(rows, lengths, queries, cache)
    weights = (w_gate, w_up, w_down)
    pieces = [rows] + [trade(rows, partners) for partners in near[:2]]
    pieces[1], attended = lax.optimization_barrier((pieces[1], attended))
    pieces.append(jnp.concatenate([diagonal, trade(arrived, near[2])], axis=0))
    held, attended = lax.optimization_barrier((rows, attended))
    pieces += [trade(piece, core) for piece in [held] + pieces[1:]]

    outputs = experts(rows, pieces, routes.shape[1], gain, weights)
    own, other = outputs[:4], outputs[4:]
    sums = [mine + trade(theirs, core).astype(jnp.float32) for mine, theirs in zip(own[1:], other[1:])]
    half = rows.shape[0] // 2
    backs = [trade(part.astype(jnp.bfloat16), partners) for part, partners in zip(sums[:2], near[:2])]
    both = sums[2].astype(jnp.bfloat16)
    back_far = trade(both[half:], near[2])
    back_near = trade(both[:half], near[2])
    total = own[0] + trade(other[0], core).astype(jnp.float32)
    attention_out = attended.reshape(1, -1)
    back_far, attention_out = lax.optimization_barrier((back_far, attention_out))
    for back in backs:
        total = total + back.astype(jnp.float32)
    send = (total[half:] + back_far.astype(jnp.float32)).astype(jnp.bfloat16)
    total = total[:half] + back_near.astype(jnp.float32)
    for index, partners in enumerate(reversed(far)):
        if index:
            half = total.shape[0] // 2
            send, total = total[half:].astype(jnp.bfloat16), total[:half]
        total = total + trade(send, partners).astype(jnp.float32)
    moe_out = total.astype(jnp.bfloat16)
    moe_out = total.astype(jnp.bfloat16)

    return (moe_out, attention_out)


def solution(mesh):
    in_specs = (
        P(("grp", "node"), None),
        P(("grp", "node"), None),
        P(("grp", "node"), None),
        P(),
        P("node", None, None),
        P("node", None, None),
        P("node", None, None),
        P(("grp", "node"), None, None),
        P(("grp", "node"), None, None),
        P(("grp", "node")),
    )
    out_specs = (P(("grp", "node"), None), P(("grp", "node"), None))
    return jax.shard_map(
        per_device, mesh=mesh, in_specs=in_specs, out_specs=out_specs, check_vma=False
    )
```

```python
import functools

import jax
import jax.numpy as jnp
from jax import lax
from jax.experimental import pallas as pl
from jax.experimental.pallas import tpu as pltpu
from jax.sharding import PartitionSpec as P

SPLIT = 4
CHUNK = 1024
VALUE_DIM = 512
LANES = 128
VMEM_LIMIT = 24 * 1024 * 1024


norm_eps = 1e-06
route_scale = 2.5
softmax_scale = 192.0 ** (-0.5)


def exchange_steps(node_count):
    nodes = range(node_count)
    far = [[node ^ (1 << bit) for node in nodes] for bit in reversed(range(3, node_count.bit_length() - 1))]
    near = [[node ^ masks[node % 2] for node in nodes] for masks in ((2, 4), (4, 2), (6, 6))]
    return far, near, [node ^ 1 for node in nodes]


def trade(value, partners):
    return lax.ppermute(value, "node", list(enumerate(partners)))


def in_hbm(array):
    return pltpu.with_memory_space_constraint(array, pltpu.HBM)


def pack_kernel(tokens_hbm, routes_hbm, gates_hbm, rows_ref, tokens_ref, routes_ref, gates_ref, sem):
    sources, targets = (routes_hbm, gates_hbm, tokens_hbm), (routes_ref, gates_ref, tokens_ref)
    copies = [
        pltpu.make_async_copy(source, target, sem.at[index])
        for index, (source, target) in enumerate(zip(sources, targets))
    ]
    for copy in copies:
        copy.start()
    count, width = tokens_ref.shape
    picks = routes_ref.shape[0]
    copies[0].wait()
    copies[1].wait()
    gates = gates_ref[...]
    mixing = route_scale * gates / jnp.sum(gates, axis=0, keepdims=True)
    high = mixing.astype(jnp.bfloat16).astype(jnp.float32)
    parts = [routes_ref[...].astype(jnp.float32), high, mixing - high]
    row = lax.broadcasted_iota(jnp.int32, (count, count), 0)
    diagonal = row == lax.broadcasted_iota(jnp.int32, (count, count), 1)
    lane = lax.broadcasted_iota(jnp.int32, (count, LANES), 1)
    notes = jnp.zeros((count, LANES), jnp.float32)
    for part, values in enumerate(parts):
        for pick in range(picks):
            spread = jnp.broadcast_to(values[pick : pick + 1], (count, count))
            column = jnp.sum(jnp.where(diagonal, spread, 0.0), axis=1, keepdims=True)
            notes = jnp.where(lane == part * picks + pick, column, notes)
    rows_ref[:, width:] = notes.astype(jnp.bfloat16)
    copies[2].wait()
    rows_ref[:, :width] = tokens_ref[...]


def pack(tokens, routes, gates):
    count, width = tokens.shape
    picks = routes.shape[1]
    hbm = pl.BlockSpec(memory_space=pltpu.HBM)
    return pl.pallas_call(
        pack_kernel,
        out_shape=jax.ShapeDtypeStruct((count, width + LANES), jnp.bfloat16),
        in_specs=[hbm, hbm, hbm],
        scratch_shapes=[
            pltpu.VMEM((count, width), jnp.bfloat16),
            pltpu.VMEM((picks, count), jnp.int32),
            pltpu.VMEM((picks, count), jnp.float32),
            pltpu.SemaphoreType.DMA((3,)),
        ],
        compiler_params=pltpu.CompilerParams(vmem_limit_bytes=VMEM_LIMIT),
        name="pack",
    )(*map(in_hbm, (tokens, routes.T, gates.T)))


def join_kernel(upper_ref, lower_ref, rows_ref):
    half = upper_ref.shape[0]
    rows_ref[:half] = upper_ref[...]
    rows_ref[half:] = lower_ref[...]


def join(upper, lower):
    half, width = upper.shape
    return pl.pallas_call(
        join_kernel,
        out_shape=jax.ShapeDtypeStruct((2 * half, width), upper.dtype),
        compiler_params=pltpu.CompilerParams(vmem_limit_bytes=VMEM_LIMIT),
        cost_estimate=pl.CostEstimate(flops=4_000_000_000, bytes_accessed=500_000, transcendentals=0),
        name="join",
    )(upper, lower)


def attention_kernel(after_ref, lengths_ref, queries_ref, cache_ref, attended_ref):
    queries = queries_ref[0].T
    cached = cache_ref[0]
    scores = jnp.dot(queries, cached, preferred_element_type=jnp.float32) * softmax_scale
    position = lax.broadcasted_iota(jnp.int32, scores.shape, 1)
    scores = jnp.where(position < lengths_ref[0], scores, -jnp.inf)
    powers = jnp.exp(scores - jnp.max(scores, axis=-1, keepdims=True))
    probs = (powers / jnp.sum(powers, axis=-1, keepdims=True)).astype(jnp.bfloat16)
    attended = lax.dot_general(
        probs,
        cached[:VALUE_DIM],
        (((1,), (1,)), ((), ())),
        preferred_element_type=jnp.float32,
    )
    attended_ref[0] = attended.astype(jnp.bfloat16)


def attention(after, lengths, queries, cache):
    heads = queries.shape[1]
    queries = jnp.swapaxes(queries, 1, 2)
    cache = jnp.swapaxes(cache, 1, 2)
    vmem = pl.BlockSpec(memory_space=pltpu.VMEM)
    return pl.pallas_call(
        attention_kernel,
        out_shape=jax.ShapeDtypeStruct((1, heads, VALUE_DIM), jnp.bfloat16),
        in_specs=[pl.BlockSpec(memory_space=pl.ANY), pl.BlockSpec(memory_space=pltpu.SMEM), vmem, vmem],
        compiler_params=pltpu.CompilerParams(vmem_limit_bytes=VMEM_LIMIT),
        cost_estimate=pl.CostEstimate(flops=360_000_000, bytes_accessed=1_700_000, transcendentals=164_000),
        name="attention",
    )(after, lengths, queries, cache)


def experts_kernel(picks, count, loaded_ref, *refs):
    pieces, (gain_ref, gate_ref, up_ref, down_ref) = refs[:count], refs[count : count + 4]
    outputs = refs[count + 4 :]
    width = gate_ref.shape[1]
    rows = [piece.shape[0] for piece in pieces]
    total = sum(rows)
    padding = -total % LANES
    gate_part = jnp.zeros((total + padding, gate_ref.shape[2]), jnp.float32)
    up_part = jnp.zeros((total + padding, up_ref.shape[2]), jnp.float32)
    squares = [jnp.zeros((size, LANES), jnp.float32) for size in rows]
    for start in range(0, width, CHUNK):
        stop = min(start + CHUNK, width)
        scaled = []
        for lane in range(start, stop, LANES):
            gain = gain_ref[lane // LANES : lane // LANES + 1, :].astype(jnp.float32)
            column = []
            for index, piece in enumerate(pieces):
                part = piece[:, lane : lane + LANES].astype(jnp.float32)
                squares[index] = squares[index] + part * part
                column.append(part * gain)
            if padding:
                column.append(jnp.zeros((padding, LANES), jnp.float32))
            scaled.append(jnp.concatenate(column, axis=0).astype(jnp.bfloat16))
        scaled = jnp.concatenate(scaled, axis=1)
        gate_part += jnp.dot(scaled, gate_ref[0, start:stop, :], preferred_element_type=jnp.float32)
        up_part += jnp.dot(scaled, up_ref[0, start:stop, :], preferred_element_type=jnp.float32)
    squares = jnp.concatenate(squares, axis=0)
    inverse = lax.rsqrt(jnp.sum(squares, axis=-1, keepdims=True) / width + norm_eps)
    gate_part = gate_part[:total] * inverse
    up_part = up_part[:total] * inverse
    notes = jnp.concatenate([piece[:, width:].astype(jnp.float32) for piece in pieces], axis=0)
    replica = (lax.axis_index("node") // SPLIT).astype(jnp.float32)
    share = jnp.zeros((total, 1), jnp.float32)
    for pick in range(picks):
        weight = notes[:, picks + pick : picks + pick + 1] + notes[:, 2 * picks + pick : 2 * picks + pick + 1]
        share = share + jnp.where(notes[:, pick : pick + 1] == replica, weight, 0.0)
    hidden = gate_part / (1.0 + jnp.exp(-gate_part)) * up_part * share
    hidden = hidden.astype(jnp.bfloat16)
    if padding:
        hidden = jnp.concatenate([hidden, jnp.zeros((padding, hidden.shape[1]), hidden.dtype)], axis=0)
    for start in range(0, width, CHUNK):
        stop = min(start + CHUNK, width)
        part = jnp.dot(hidden, down_ref[0, :, start:stop], preferred_element_type=jnp.float32)
        first = 0
        for size, output in zip(rows, outputs):
            output[:, start:stop] = part[first : first + size].astype(output.dtype)
            first += size


def experts(loaded, pieces, picks, gain, weights):
    count = len(pieces)
    width = weights[0].shape[1]
    types = [jnp.float32] * (count // 2) + [jnp.bfloat16] * (count - count // 2)
    vmem = pl.BlockSpec(memory_space=pltpu.VMEM)
    return pl.pallas_call(
        functools.partial(experts_kernel, picks, count),
        out_shape=tuple(
            jax.ShapeDtypeStruct((piece.shape[0], width), kind) for piece, kind in zip(pieces, types)
        ),
        in_specs=[pl.BlockSpec(memory_space=pl.ANY)] + [vmem] * (count + 4),
        out_specs=(vmem,) * count,
        compiler_params=pltpu.CompilerParams(vmem_limit_bytes=VMEM_LIMIT),
        cost_estimate=pl.CostEstimate(flops=2_000_000_000, bytes_accessed=500_000, transcendentals=0),
        name="experts",
    )(loaded, *pieces, gain, *weights)


def per_device(tokens, routes, gates, norm_gain, w_gate, w_up, w_down, queries, cache, lengths):
    far, near, core = exchange_steps(lax.axis_size("node"))
    gain = norm_gain.reshape(-1, LANES)

    rows = pack(tokens, routes, gates)
    for partners in far[:-1]:
        rows = jnp.concatenate([rows, trade(rows, partners)], axis=0)
    arrived = trade(rows, far[-1])
    across = [far[-1][partner] for partner in near[2]]
    beside = trade(rows, near[2])
    beyond = trade(rows, across)
    rows = join(rows, arrived)
    attended = attention(rows, lengths, queries, cache)
    weights = (w_gate, w_up, w_down)
    pieces = [rows] + [trade(rows, partners) for partners in near[:2]]
    beyond, attended = lax.optimization_barrier((beyond, attended))
    pieces.append(jnp.concatenate([beside, beyond], axis=0))
    held, attended = lax.optimization_barrier((rows, attended))
    pieces += [trade(piece, core) for piece in [held] + pieces[1:]]
    outputs = experts(rows, pieces, routes.shape[1], gain, weights)
    own, other = outputs[:4], outputs[4:]
    sums = [mine + trade(theirs, core).astype(jnp.float32) for mine, theirs in zip(own[1:], other[1:])]
    half = rows.shape[0] // 2
    backs = [trade(part.astype(jnp.bfloat16), partners) for part, partners in zip(sums[:2], near[:2])]
    both = sums[2].astype(jnp.bfloat16)
    back_far = trade(both[half:], near[2])
    back_near = trade(both[:half], near[2])
    total = own[0] + trade(other[0], core).astype(jnp.float32)
    attention_out = attended.reshape(1, -1)
    back_far, attention_out = lax.optimization_barrier((back_far, attention_out))
    for back in backs:
        total = total + back.astype(jnp.float32)
    send = (total[half:] + back_far.astype(jnp.float32)).astype(jnp.bfloat16)
    total = total[:half] + back_near.astype(jnp.float32)
    for index, partners in enumerate(reversed(far)):
        if index:
            half = total.shape[0] // 2
            send, total = total[half:].astype(jnp.bfloat16), total[:half]
        total = total + trade(send, partners).astype(jnp.float32)
    moe_out = total.astype(jnp.bfloat16)
    moe_out = total.astype(jnp.bfloat16)

    return (moe_out, attention_out)


def solution(mesh):
    in_specs = (
        P(("grp", "node"), None),
        P(("grp", "node"), None),
        P(("grp", "node"), None),
        P(),
        P("node", None, None),
        P("node", None, None),
        P("node", None, None),
        P(("grp", "node"), None, None),
        P(("grp", "node"), None, None),
        P(("grp", "node")),
    )
    out_specs = (P(("grp", "node"), None), P(("grp", "node"), None))
    return jax.shard_map(
        per_device, mesh=mesh, in_specs=in_specs, out_specs=out_specs, check_vma=False
    )
```

```python
import functools

import jax
import jax.numpy as jnp
from jax import lax
from jax.experimental import pallas as pl
from jax.experimental.pallas import tpu as pltpu
from jax.sharding import PartitionSpec as P

SPLIT = 4
CHUNK = 1024
VALUE_DIM = 512
LANES = 128
VMEM_LIMIT = 24 * 1024 * 1024


norm_eps = 1e-06
route_scale = 2.5
softmax_scale = 192.0 ** (-0.5)


def exchange_steps(node_count):
    nodes = range(node_count)
    far = [[node ^ (1 << bit) for node in nodes] for bit in reversed(range(3, node_count.bit_length() - 1))]
    near = [[node ^ masks[node % 2] for node in nodes] for masks in ((2, 4), (4, 2), (6, 6))]
    return far, near, [node ^ 1 for node in nodes]


def trade(value, partners):
    return lax.ppermute(value, "node", list(enumerate(partners)))


def in_hbm(array):
    return pltpu.with_memory_space_constraint(array, pltpu.HBM)


def pack_kernel(tokens_hbm, routes_hbm, gates_hbm, rows_ref, tokens_ref, routes_ref, gates_ref, sem):
    sources, targets = (routes_hbm, gates_hbm, tokens_hbm), (routes_ref, gates_ref, tokens_ref)
    copies = [
        pltpu.make_async_copy(source, target, sem.at[index])
        for index, (source, target) in enumerate(zip(sources, targets))
    ]
    for copy in copies:
        copy.start()
    count, width = tokens_ref.shape
    picks = routes_ref.shape[0]
    copies[0].wait()
    copies[1].wait()
    gates = gates_ref[...]
    mixing = route_scale * gates / jnp.sum(gates, axis=0, keepdims=True)
    high = mixing.astype(jnp.bfloat16).astype(jnp.float32)
    parts = [routes_ref[...].astype(jnp.float32), high, mixing - high]
    row = lax.broadcasted_iota(jnp.int32, (count, count), 0)
    diagonal = row == lax.broadcasted_iota(jnp.int32, (count, count), 1)
    lane = lax.broadcasted_iota(jnp.int32, (count, LANES), 1)
    notes = jnp.zeros((count, LANES), jnp.float32)
    for part, values in enumerate(parts):
        for pick in range(picks):
            spread = jnp.broadcast_to(values[pick : pick + 1], (count, count))
            column = jnp.sum(jnp.where(diagonal, spread, 0.0), axis=1, keepdims=True)
            notes = jnp.where(lane == part * picks + pick, column, notes)
    rows_ref[:, width:] = notes.astype(jnp.bfloat16)
    copies[2].wait()
    rows_ref[:, :width] = tokens_ref[...]


def pack(tokens, routes, gates):
    count, width = tokens.shape
    picks = routes.shape[1]
    hbm = pl.BlockSpec(memory_space=pltpu.HBM)
    return pl.pallas_call(
        pack_kernel,
        out_shape=jax.ShapeDtypeStruct((count, width + LANES), jnp.bfloat16),
        in_specs=[hbm, hbm, hbm],
        scratch_shapes=[
            pltpu.VMEM((count, width), jnp.bfloat16),
            pltpu.VMEM((picks, count), jnp.int32),
            pltpu.VMEM((picks, count), jnp.float32),
            pltpu.SemaphoreType.DMA((3,)),
        ],
        compiler_params=pltpu.CompilerParams(vmem_limit_bytes=VMEM_LIMIT),
        name="pack",
    )(*map(in_hbm, (tokens, routes.T, gates.T)))


def join_kernel(upper_ref, lower_ref, rows_ref):
    half = upper_ref.shape[0]
    rows_ref[:half] = upper_ref[...]
    rows_ref[half:] = lower_ref[...]


def join(upper, lower):
    half, width = upper.shape
    return pl.pallas_call(
        join_kernel,
        out_shape=jax.ShapeDtypeStruct((2 * half, width), upper.dtype),
        compiler_params=pltpu.CompilerParams(vmem_limit_bytes=VMEM_LIMIT),
        cost_estimate=pl.CostEstimate(flops=4_000_000_000, bytes_accessed=500_000, transcendentals=0),
        name="join",
    )(upper, lower)


def attention_kernel(after_ref, lengths_ref, queries_ref, cache_ref, attended_ref):
    queries = queries_ref[0].T
    cached = cache_ref[0]
    scores = jnp.dot(queries, cached, preferred_element_type=jnp.float32) * softmax_scale
    position = lax.broadcasted_iota(jnp.int32, scores.shape, 1)
    scores = jnp.where(position < lengths_ref[0], scores, -jnp.inf)
    powers = jnp.exp(scores - jnp.max(scores, axis=-1, keepdims=True))
    probs = (powers / jnp.sum(powers, axis=-1, keepdims=True)).astype(jnp.bfloat16)
    attended = lax.dot_general(
        probs,
        cached[:VALUE_DIM],
        (((1,), (1,)), ((), ())),
        preferred_element_type=jnp.float32,
    )
    attended_ref[0] = attended.astype(jnp.bfloat16)


def attention(after, lengths, queries, cache):
    heads = queries.shape[1]
    queries = jnp.swapaxes(queries, 1, 2)
    cache = jnp.swapaxes(cache, 1, 2)
    vmem = pl.BlockSpec(memory_space=pltpu.VMEM)
    return pl.pallas_call(
        attention_kernel,
        out_shape=jax.ShapeDtypeStruct((1, heads, VALUE_DIM), jnp.bfloat16),
        in_specs=[pl.BlockSpec(memory_space=pl.ANY), pl.BlockSpec(memory_space=pltpu.SMEM), vmem, vmem],
        compiler_params=pltpu.CompilerParams(vmem_limit_bytes=VMEM_LIMIT),
        cost_estimate=pl.CostEstimate(flops=360_000_000, bytes_accessed=1_700_000, transcendentals=164_000),
        name="attention",
    )(after, lengths, queries, cache)


def experts_kernel(picks, count, loaded_ref, *refs):
    pieces, (gain_ref, gate_ref, up_ref, down_ref) = refs[:count], refs[count : count + 4]
    outputs = refs[count + 4 :]
    width = gate_ref.shape[1]
    rows = [piece.shape[0] for piece in pieces]
    total = sum(rows)
    padding = -total % LANES
    gate_part = jnp.zeros((total + padding, gate_ref.shape[2]), jnp.float32)
    up_part = jnp.zeros((total + padding, up_ref.shape[2]), jnp.float32)
    squares = [jnp.zeros((size, LANES), jnp.float32) for size in rows]
    for start in range(0, width, CHUNK):
        stop = min(start + CHUNK, width)
        scaled = []
        for lane in range(start, stop, LANES):
            gain = gain_ref[lane // LANES : lane // LANES + 1, :].astype(jnp.float32)
            column = []
            for index, piece in enumerate(pieces):
                part = piece[:, lane : lane + LANES].astype(jnp.float32)
                squares[index] = squares[index] + part * part
                column.append(part * gain)
            if padding:
                column.append(jnp.zeros((padding, LANES), jnp.float32))
            scaled.append(jnp.concatenate(column, axis=0).astype(jnp.bfloat16))
        scaled = jnp.concatenate(scaled, axis=1)
        gate_part += jnp.dot(scaled, gate_ref[0, start:stop, :], preferred_element_type=jnp.float32)
        up_part += jnp.dot(scaled, up_ref[0, start:stop, :], preferred_element_type=jnp.float32)
    squares = jnp.concatenate(squares, axis=0)
    inverse = lax.rsqrt(jnp.sum(squares, axis=-1, keepdims=True) / width + norm_eps)
    gate_part = gate_part[:total] * inverse
    up_part = up_part[:total] * inverse
    notes = jnp.concatenate([piece[:, width:].astype(jnp.float32) for piece in pieces], axis=0)
    replica = (lax.axis_index("node") // SPLIT).astype(jnp.float32)
    share = jnp.zeros((total, 1), jnp.float32)
    for pick in range(picks):
        weight = notes[:, picks + pick : picks + pick + 1] + notes[:, 2 * picks + pick : 2 * picks + pick + 1]
        share = share + jnp.where(notes[:, pick : pick + 1] == replica, weight, 0.0)
    hidden = gate_part / (1.0 + jnp.exp(-gate_part)) * up_part * share
    hidden = hidden.astype(jnp.bfloat16)
    if padding:
        hidden = jnp.concatenate([hidden, jnp.zeros((padding, hidden.shape[1]), hidden.dtype)], axis=0)
    for start in range(0, width, CHUNK):
        stop = min(start + CHUNK, width)
        part = jnp.dot(hidden, down_ref[0, :, start:stop], preferred_element_type=jnp.float32)
        first = 0
        for size, output in zip(rows, outputs):
            output[:, start:stop] = part[first : first + size].astype(output.dtype)
            first += size


def experts(loaded, pieces, picks, gain, weights):
    count = len(pieces)
    width = weights[0].shape[1]
    types = [jnp.float32] * (count // 2) + [jnp.bfloat16] * (count - count // 2)
    vmem = pl.BlockSpec(memory_space=pltpu.VMEM)
    return pl.pallas_call(
        functools.partial(experts_kernel, picks, count),
        out_shape=tuple(
            jax.ShapeDtypeStruct((piece.shape[0], width), kind) for piece, kind in zip(pieces, types)
        ),
        in_specs=[pl.BlockSpec(memory_space=pl.ANY)] + [vmem] * (count + 4),
        out_specs=(vmem,) * count,
        compiler_params=pltpu.CompilerParams(vmem_limit_bytes=VMEM_LIMIT),
        cost_estimate=pl.CostEstimate(flops=2_000_000_000, bytes_accessed=500_000, transcendentals=0),
        name="experts",
    )(loaded, *pieces, gain, *weights)


def per_device(tokens, routes, gates, norm_gain, w_gate, w_up, w_down, queries, cache, lengths):
    far, near, core = exchange_steps(lax.axis_size("node"))
    gain = norm_gain.reshape(-1, LANES)

    rows = pack(tokens, routes, gates)
    for partners in far[:-1]:
        rows = jnp.concatenate([rows, trade(rows, partners)], axis=0)
    arrived = trade(rows, far[-1])
    across = [far[-1][partner] for partner in near[2]]
    beside = trade(rows, near[2])
    beyond = trade(rows, across)
    rows = join(rows, arrived)
    attended = attention(rows, lengths, queries, cache)
    weights = (w_gate, w_up, w_down)
    pieces = [rows] + [trade(rows, partners) for partners in near[:2]]
    beside, attended = lax.optimization_barrier((beside, attended))
    pieces.append(jnp.concatenate([beside, beyond], axis=0))
    pieces += [trade(piece, core) for piece in pieces]
    outputs = experts(rows, pieces, routes.shape[1], gain, weights)
    own, other = outputs[:4], outputs[4:]
    sums = [mine + trade(theirs, core).astype(jnp.float32) for mine, theirs in zip(own[1:], other[1:])]
    half = rows.shape[0] // 2
    backs = [trade(part.astype(jnp.bfloat16), partners) for part, partners in zip(sums[:2], near[:2])]
    both = sums[2].astype(jnp.bfloat16)
    back_far = trade(both[half:], near[2])
    back_near = trade(both[:half], near[2])
    total = own[0] + trade(other[0], core).astype(jnp.float32)
    attention_out = attended.reshape(1, -1)
    back_far, attention_out = lax.optimization_barrier((back_far, attention_out))
    for back in backs:
        total = total + back.astype(jnp.float32)
    send = (total[half:] + back_far.astype(jnp.float32)).astype(jnp.bfloat16)
    total = total[:half] + back_near.astype(jnp.float32)
    for index, partners in enumerate(reversed(far)):
        if index:
            half = total.shape[0] // 2
            send, total = total[half:].astype(jnp.bfloat16), total[:half]
        total = total + trade(send, partners).astype(jnp.float32)
    moe_out = total.astype(jnp.bfloat16)
    moe_out = total.astype(jnp.bfloat16)

    return (moe_out, attention_out)


def solution(mesh):
    in_specs = (
        P(("grp", "node"), None),
        P(("grp", "node"), None),
        P(("grp", "node"), None),
        P(),
        P("node", None, None),
        P("node", None, None),
        P("node", None, None),
        P(("grp", "node"), None, None),
        P(("grp", "node"), None, None),
        P(("grp", "node")),
    )
    out_specs = (P(("grp", "node"), None), P(("grp", "node"), None))
    return jax.shard_map(
        per_device, mesh=mesh, in_specs=in_specs, out_specs=out_specs, check_vma=False
    )
```
